512 devices in a mesh: ba: 32 (over z, y_lo), dev: 16 (over y_hi, x, core).
Axes of the slice: x: 4, y: 8 (y_hi: 2, y_lo: 4; y = y_hi * 4 + y_lo), z: 8, core: 2. Of those that a mesh axis runs over, the one named last changes fastest.
Arguments:
- factors: bfloat16 [64, 512, 1024], P('ba', 'dev'), may hold values from -0.1875 to 0.1875
- amplitudes: bfloat16 [64, 512, 512], P(None, 'dev'), may hold values from -0.375 to 0.375
- pair_order: int32 [64], replicated, may hold values from 0 to 63, each once
- occ_bin: int32 [8], replicated, may hold values from 0 to 127
- vir_bin: int32 [64], replicated, may hold values from 0 to 127
- levels: float32 [128], replicated, may hold values from 0.1 to 0.8
Outputs:
- update: float32 [64, 4096], P('ba', 'dev')
The draws below stay inside these ranges and needn't reach their ends.
Inputs may be any that keep to these rules, and one draw needn't show every extreme that they name: `pair_order`: each value appears once; entry k names the ordered occupied pair (value // 8, value % 8). `occ_bin`: orbital i has energy minus levels at its bin. `vir_bin`: window virtual a has energy levels at its bin.
All inputs are finite; a program needn't handle non-finite values.
Results may differ from the reference program's by a relative error of at most 0.0029.
Values may be sent and summed in bfloat16 or wider, within the bound.
No kernel may reach another device: no remote copies, remote signals or barrier semaphores. Data moves between devices by JAX's collectives and lax.ppermute only.
A program may use at most 64 MiB of HBM per device.

```python
import jax
import jax.numpy as jnp
from jax import lax

V = 512
NAUX = 1024
NOCC = 8
LEVELS = 128
NW = 64
P_SIZE = 64


def touch_ends(entries, own_key, low, largest):
    longest = entries.shape.index(max(entries.shape))
    spots = []
    for shift in (0, 1):
        where = [jax.random.randint(jax.random.fold_in(own_key, axis), (), 0, length) for axis, length in enumerate(entries.shape)]
        where[longest] = (where[longest] + shift) % entries.shape[longest]
        spots.append(tuple(where))
    return entries.at[spots[0]].set(low).at[spots[1]].set(largest)


def steps_of(key, dims, pieces, least, largest):
    loudness, own = 1.0, jax.random.fold_in(key, 6)
    for axis_at, blocks in pieces:
        draws = jnp.exp(jax.random.uniform(jax.random.fold_in(own, axis_at), (blocks,), jnp.float32, least / len(pieces), largest / len(pieces)))
        loudness = loudness * jnp.repeat(draws, dims[axis_at] // blocks).reshape([-1 if axis == axis_at else 1 for axis in range(len(dims))])
    return loudness


def bell_draw(rng, shape, deviation, bound, shards=(), kind=jnp.bfloat16):
    factor_of = steps_of(rng, shape, shards, -0.22, 0.18) if shards else 1.0
    array = jax.random.normal(rng, shape, jnp.float32) * deviation * factor_of
    return jnp.minimum(jnp.maximum(array, -bound), bound).astype(kind)


def setup_inputs(seed: int = 0) -> dict:
    splits = jax.random.split(jax.random.key(seed), 7)
    factors = bell_draw(splits[0], (NW, V, NAUX), NAUX ** -0.5, 0.1875, ((0, 32), (1, 16)))
    amplitudes = bell_draw(splits[1], (P_SIZE, V, V), (V * V // NAUX) ** -0.5, 0.375, ((1, 16),))
    pair_order = jax.random.permutation(splits[2], P_SIZE).astype(jnp.int32)
    occ_bin = touch_ends(jax.random.randint(splits[3], (NOCC,), 0, LEVELS), jax.random.fold_in(splits[3], 1), 0, LEVELS - 1).astype(jnp.int32)
    vir_bin = touch_ends(jax.random.randint(splits[4], (NW,), 0, LEVELS), jax.random.fold_in(splits[4], 1), 0, LEVELS - 1).astype(jnp.int32)
    levels = jnp.clip(jax.random.uniform(splits[5], (LEVELS,), jnp.float32, 0.1, 0.8), 0.1, 0.8)
    return {"factors": factors, "amplitudes": amplitudes, "pair_order": pair_order, "occ_bin": occ_bin, "vir_bin": vir_bin, "levels": levels}


level_shift = 0.3


def reference(factors, amplitudes, pair_order, occ_bin, vir_bin, levels):
    flat_rows = factors.reshape(NW * V, NAUX)
    flat_amps = amplitudes.reshape(P_SIZE, V * V)

    def one_column(slab):
        integrals = lax.dot_general(flat_rows, slab, (((1,), (1,)), ((), ())), preferred_element_type=jnp.float32)
        integrals = integrals.astype(jnp.bfloat16).reshape(NW, V * V)
        return lax.dot_general(integrals, flat_amps, (((1,), (1,)), ((), ())), preferred_element_type=jnp.float32)

    ladder = lax.map(one_column, factors)
    counter = jnp.arange(P_SIZE, dtype=jnp.int32)
    swapped = (pair_order % NOCC) * NOCC + pair_order // NOCC
    matches = swapped[:, None] == pair_order[None, :]
    partner = jnp.sum(jnp.where(matches, counter[None, :], 0), axis=1).astype(jnp.int32)
    total = ladder + jnp.transpose(ladder, (1, 0, 2))[:, :, partner]
    virtual_energy = levels[vir_bin]
    occupied_energy = -levels[occ_bin]
    pair_energy = occupied_energy[pair_order // NOCC] + occupied_energy[pair_order % NOCC]
    denominator = virtual_energy[:, None, None] + virtual_energy[None, :, None] - pair_energy[None, None, :] + level_shift
    return (total / denominator).reshape(NW, NW * P_SIZE)
```

```python
import functools

import jax
import jax.numpy as jnp
from jax import lax
from jax.experimental import pallas as pl
from jax.experimental.pallas import tpu as pltpu
from jax.sharding import Mesh
from jax.sharding import PartitionSpec as P

NOCC = 8
AXES = ("z", "yl", "yh", "x", "c")
SIZES = (8, 4, 2, 4, 2)
BA = ("z", "yl")
DEV = ("yh", "x", "c")
GROUP = ("yl", "yh", "x", "c")
level_shift = 0.3
CSTEP = 4


def lookup(indices, table):
    choices_range = jnp.arange(table.shape[0], dtype=jnp.int32)
    return jnp.sum(
        jnp.where(indices[:, None] == choices_range[None, :], table[None, :], 0.0), axis=1
    )


def ladder_kernel(amps_ref, right_ref, left_ref, out_ref, bmat, xs, acc):
    step = pl.program_id(0)

    @pl.when(step == 0)
    def _():
        acc[...] = jnp.zeros_like(acc)
        for yl in range(4):
            for r in range(2):
                for yh in range(2):
                    for x in range(4):
                        for c in range(2):
                            d = ((yh * 4 + x) * 2 + c) * 32
                            b = yl * 2 + r
                            bmat[d : d + 32, b * 256 : (b + 1) * 256] = right_ref[c, x, yh, yl, r]

    amps = amps_ref[...].reshape(CSTEP * 64, 512)
    for b in range(8):
        prod = jnp.dot(
            amps, bmat[:, b * 256 : (b + 1) * 256], preferred_element_type=jnp.float32
        ).astype(jnp.bfloat16)
        for cc in range(CSTEP):
            xs[cc, b * 64 : (b + 1) * 64, :] = prod[cc * 64 : (cc + 1) * 64]
    total = acc[...]
    for cc in range(CSTEP):
        total += lax.dot_general(
            xs[cc], left_ref[cc], (((1,), (1,)), ((), ())), preferred_element_type=jnp.float32
        )
    acc[...] = total

    @pl.when(step == pl.num_programs(0) - 1)
    def _():
        for yl in range(4):
            w = acc[yl * 128 : (yl + 1) * 128, :].T
            for ac in range(16):
                out_ref[yl * 16 + ac, 0:4, :] = w[ac * 4 : ac * 4 + 4, :]
            c1, i2 = yl // 2, yl % 2
            for big in range(8):
                for yl1 in range(4):
                    out_ref[(yl1 * 8 + big) * 2 + c1, 4 + 2 * i2 : 6 + 2 * i2, :] = w[
                        8 * big + 2 * yl1 : 8 * big + 2 * yl1 + 2, :
                    ]


def ladder_parts(amps, right, left):
    return pl.pallas_call(
        ladder_kernel,
        grid=(32 // CSTEP,),
        in_specs=[
            pl.BlockSpec((CSTEP, 64, 512), lambda i: (i, 0, 0)),
            pl.BlockSpec((2, 4, 2, 4, 2, 32, 256), lambda i: (0,) * 7),
            pl.BlockSpec((CSTEP, 64, 256), lambda i: (i, 0, 0)),
        ],
        out_specs=pl.BlockSpec((64, 8, 128), lambda i: (0, 0, 0)),
        out_shape=jax.ShapeDtypeStruct((64, 8, 128), jnp.float32),
        scratch_shapes=[
            pltpu.VMEM((512, 2048), jnp.bfloat16),
            pltpu.VMEM((CSTEP, 512, 256), jnp.bfloat16),
            pltpu.VMEM((512, 64), jnp.float32),
        ],
        compiler_params=pltpu.CompilerParams(
            dimension_semantics=("arbitrary",), vmem_limit_bytes=32 * 1024 * 1024
        ),
        cost_estimate=pl.CostEstimate(
            flops=2 * 2048 * 512 * 2048 + 2 * 64 * 64 * 8 * 8192,
            bytes_accessed=6 * 1024 * 1024,
            transcendentals=0,
        ),
    )(amps, right, left)


def swap_pairs():
    pairs = []
    for z in range(8):
        for yl in range(4):
            for big in range(8):
                for c in range(2):
                    pairs.append((((z * 4 + yl) * 8 + big) * 2 + c, ((big * 4 + yl) * 8 + z) * 2 + c))
    return pairs


def per_device(factors, amplitudes, pair_order, occ_bin, vir_bin, levels):
    quarters = factors.reshape(64, 4, 256).transpose(1, 0, 2)
    quarters = jnp.broadcast_to(quarters[None], (2, 4, 64, 256)).reshape(8, 64, 256)
    rows = lax.all_to_all(quarters, ("yh", "yl"), 0, 0, tiled=True)
    own = lax.dynamic_slice_in_dim(rows, lax.axis_index("yh") * 4, 4)
    everyone = jnp.broadcast_to(rows.reshape(1, 512, 256), (4, 512, 256))
    right = lax.all_to_all(everyone, "x", 0, 0, tiled=True)
    right = lax.all_gather(right, "c", axis=0, tiled=False)
    right = right.reshape(2, 4, 2, 4, 2, 32, 256)
    own = jnp.broadcast_to(own.reshape(1, 256, 256), (8, 256, 256))
    left = lax.all_to_all(own, "z", 0, 0, tiled=True)
    left = left.reshape(64, 32, 256).transpose(1, 0, 2)
    amps = amplitudes.transpose(1, 0, 2)
    parts = ladder_parts(amps, right, left)
    parts = lax.all_to_all(parts, GROUP, 0, 0, tiled=True)
    summed = parts.sum(axis=0)
    direct = summed[:4].reshape(4, 2, 64)
    flipped = lax.ppermute(summed[4:], AXES, swap_pairs())
    flipped = flipped.reshape(2, 2, 2, 64).transpose(0, 2, 1, 3).reshape(4, 2, 64)

    swapped = pair_order % NOCC * NOCC + pair_order // NOCC
    matches = swapped[:, None] == pair_order[None, :]
    partnered = jnp.sum(
        jnp.where(matches[None, None], flipped[:, :, None, :], 0.0), axis=-1
    )
    total = (direct + partnered).transpose(1, 0, 2)

    virtual_energy = lookup(vir_bin, levels)
    occupied_energy = -lookup(occ_bin, levels)
    pair_energy = lookup(pair_order // NOCC, occupied_energy) + lookup(
        pair_order % NOCC, occupied_energy
    )
    left_energy = lax.dynamic_slice_in_dim(virtual_energy, lax.axis_index(DEV) * 4, 4)
    right_energy = lax.dynamic_slice_in_dim(virtual_energy, lax.axis_index(BA) * 2, 2)
    denominator = (
        right_energy[:, None, None]
        + left_energy[None, :, None]
        - pair_energy[None, None, :]
        + level_shift
    )
    return (total / denominator).reshape(2, 256)


def solution(mesh):
    finer = Mesh(mesh.devices.reshape(SIZES), AXES)
    return jax.shard_map(
        per_device,
        mesh=finer,
        in_specs=(P(BA, DEV, None), P(None, DEV, None), P(), P(), P(), P()),
        out_specs=P(BA, DEV),
        check_vma=False,
    )
```

```python
import functools

import jax
import jax.numpy as jnp
from jax import lax
from jax.experimental import pallas as pl
from jax.experimental.pallas import tpu as pltpu
from jax.sharding import Mesh
from jax.sharding import PartitionSpec as P

NOCC = 8
AXES = ("z", "yl", "yh", "x", "c")
SIZES = (8, 4, 2, 4, 2)
BA = ("z", "yl")
DEV = ("yh", "x", "c")
GROUP = ("yl", "yh", "x", "c")
level_shift = 0.3
DSTEP = 4
LSTEP = 8


def lookup(indices, table):
    choices_range = jnp.arange(table.shape[0], dtype=jnp.int32)
    return jnp.sum(
        jnp.where(indices[:, None] == choices_range[None, :], table[None, :], 0.0), axis=1
    )


def product_kernel(where_ref, own_ref, other_ref, r0_ref, rp_ref, rm_ref, rt_ref, out_ref, bmat):
    x, c = where_ref[0], where_ref[1]

    @pl.when(pl.program_id(0) == 0)
    def _():
        for ref, shift in ((r0_ref, 0), (rp_ref, 3), (rm_ref, 1), (rt_ref, 2)):
            source = (x + shift) & 3
            for yh in range(2):
                for yl in range(4):
                    for cc in range(2):
                        for r in range(2):
                            d = pl.multiple_of((yh * 4 + source) * 64 + cc * 32, 32)
                            b = yl * 2 + r
                            bmat[pl.ds(d, 32), b * 128 : (b + 1) * 128] = ref[
                                (yh * 4 + yl) * 2 + cc, r * 32 : r * 32 + 32, :
                            ]

    for amps_ref, cc in ((own_ref, c), (other_ref, 1 - c)):
        amps = amps_ref[...].reshape(DSTEP * 64, 512)
        lanes = pl.ds(pl.multiple_of(cc * 128, 128), 128)
        for bb in range(4):
            prod = jnp.dot(
                amps, bmat[:, bb * 256 : (bb + 1) * 256], preferred_element_type=jnp.float32
            ).astype(jnp.bfloat16)
            for dd in range(DSTEP):
                for r in range(2):
                    b = bb * 2 + r
                    out_ref[dd, b * 64 : (b + 1) * 64, lanes] = prod[
                        dd * 64 : (dd + 1) * 64, r * 128 : (r + 1) * 128
                    ]


def products(where, own, other, rights):
    block = pl.BlockSpec((DSTEP, 64, 512), lambda i, w: (i, 0, 0))
    whole = pl.BlockSpec((16, 64, 128), lambda i, w: (0, 0, 0))
    return pl.pallas_call(
        product_kernel,
        grid_spec=pltpu.PrefetchScalarGridSpec(
            num_scalar_prefetch=1,
            grid=(32 // DSTEP,),
            in_specs=[block, block, whole, whole, whole, whole],
            out_specs=pl.BlockSpec((DSTEP, 512, 256), lambda i, w: (i, 0, 0)),
            scratch_shapes=[pltpu.VMEM((512, 1024), jnp.bfloat16)],
        ),
        out_shape=jax.ShapeDtypeStruct((32, 512, 256), jnp.bfloat16),
        compiler_params=pltpu.CompilerParams(
            dimension_semantics=("arbitrary",), vmem_limit_bytes=56 * 1024 * 1024
        ),
        cost_estimate=pl.CostEstimate(
            flops=2 * 4096 * 512 * 1024, bytes_accessed=14 * 1024 * 1024, transcendentals=0
        ),
    )(where, own, other, *rights)


def ladder_kernel(prod_ref, left_ref, out_ref, acc):
    step = pl.program_id(0)

    @pl.when(step == 0)
    def _():
        acc[...] = jnp.zeros_like(acc)

    total = acc[...]
    for dd in range(LSTEP):
        total += lax.dot_general(
            prod_ref[dd], left_ref[dd], (((1,), (1,)), ((), ())), preferred_element_type=jnp.float32
        )
    acc[...] = total

    @pl.when(step == pl.num_programs(0) - 1)
    def _():
        for yl in range(4):
            w = acc[yl * 128 : (yl + 1) * 128, :].T
            for ac in range(16):
                out_ref[yl * 16 + ac, 0:4, :] = w[ac * 4 : ac * 4 + 4, :]
            c1, i2 = yl // 2, yl % 2
            for big in range(8):
                for yl1 in range(4):
                    out_ref[(yl1 * 8 + big) * 2 + c1, 4 + 2 * i2 : 6 + 2 * i2, :] = w[
                        8 * big + 2 * yl1 : 8 * big + 2 * yl1 + 2, :
                    ]


def ladder_parts(prods, left):
    return pl.pallas_call(
        ladder_kernel,
        grid=(32 // LSTEP,),
        in_specs=[
            pl.BlockSpec((LSTEP, 512, 256), lambda i: (i, 0, 0)),
            pl.BlockSpec((LSTEP, 64, 256), lambda i: (i, 0, 0)),
        ],
        out_specs=pl.BlockSpec((64, 8, 128), lambda i: (0, 0, 0)),
        out_shape=jax.ShapeDtypeStruct((64, 8, 128), jnp.float32),
        scratch_shapes=[pltpu.VMEM((512, 64), jnp.float32)],
        compiler_params=pltpu.CompilerParams(
            dimension_semantics=("arbitrary",), vmem_limit_bytes=56 * 1024 * 1024
        ),
        cost_estimate=pl.CostEstimate(
            flops=2 * 64 * 64 * 8 * 8192, bytes_accessed=9 * 1024 * 1024, transcendentals=0
        ),
    )(prods, left)


def swap_pairs():
    pairs = []
    for z in range(8):
        for yl in range(4):
            for big in range(8):
                for c in range(2):
                    pairs.append((((z * 4 + yl) * 8 + big) * 2 + c, ((big * 4 + yl) * 8 + z) * 2 + c))
    return pairs


def per_device(factors, amplitudes, pair_order, occ_bin, vir_bin, levels):
    eighths = factors.reshape(64, 8, 128).transpose(1, 0, 2)
    eighths = jnp.broadcast_to(eighths[None], (2, 8, 64, 128)).reshape(16, 64, 128)
    rows = lax.all_to_all(eighths, ("yh", "yl", "c"), 0, 0, tiled=True)
    amps = amplitudes.transpose(1, 0, 2)
    amps_other = lax.ppermute(amps, "c", [(0, 1), (1, 0)])
    own = lax.dynamic_slice_in_dim(rows, lax.axis_index("yh") * 8, 8)
    own = jnp.broadcast_to(own.reshape(1, 512, 128), (8, 512, 128))
    left = lax.all_to_all(own, "z", 0, 0, tiled=True)
    left = left.reshape(8, 4, 2, 2, 32, 128).transpose(4, 0, 1, 3, 2, 5).reshape(32, 64, 256)
    rights = [rows] + [
        lax.ppermute(rows, "x", [(i, (i + s) % 4) for i in range(4)]) for s in (1, 3, 2)
    ]
    where = jnp.stack([lax.axis_index("x"), lax.axis_index("c")]).astype(jnp.int32)
    prods = products(where, amps, amps_other, rights)
    parts = ladder_parts(prods, left)
    parts = lax.all_to_all(parts, GROUP, 0, 0, tiled=True)
    summed = parts.sum(axis=0)
    direct = summed[:4].reshape(4, 2, 64)
    flipped = lax.ppermute(summed[4:], AXES, swap_pairs())
    flipped = flipped.reshape(2, 2, 2, 64).transpose(0, 2, 1, 3).reshape(4, 2, 64)

    swapped = pair_order % NOCC * NOCC + pair_order // NOCC
    matches = swapped[:, None] == pair_order[None, :]
    partnered = jnp.sum(
        jnp.where(matches[None, None], flipped[:, :, None, :], 0.0), axis=-1
    )
    total = (direct + partnered).transpose(1, 0, 2)

    virtual_energy = lookup(vir_bin, levels)
    occupied_energy = -lookup(occ_bin, levels)
    pair_energy = lookup(pair_order // NOCC, occupied_energy) + lookup(
        pair_order % NOCC, occupied_energy
    )
    left_energy = lax.dynamic_slice_in_dim(virtual_energy, lax.axis_index(DEV) * 4, 4)
    right_energy = lax.dynamic_slice_in_dim(virtual_energy, lax.axis_index(BA) * 2, 2)
    denominator = (
        right_energy[:, None, None]
        + left_energy[None, :, None]
        - pair_energy[None, None, :]
        + level_shift
    )
    return (total / denominator).reshape(2, 256)


def solution(mesh):
    finer = Mesh(mesh.devices.reshape(SIZES), AXES)
    return jax.shard_map(
        per_device,
        mesh=finer,
        in_specs=(P(BA, DEV, None), P(None, DEV, None), P(), P(), P(), P()),
        out_specs=P(BA, DEV),
        check_vma=False,
    )
```

```python
import functools

import jax
import jax.numpy as jnp
from jax import lax
from jax.experimental import pallas as pl
from jax.experimental.pallas import tpu as pltpu
from jax.sharding import Mesh
from jax.sharding import PartitionSpec as P

NOCC = 8
AXES = ("z", "yl", "yh", "x", "c")
SIZES = (8, 4, 2, 4, 2)
BA = ("z", "yl")
DEV = ("yh", "x", "c")
GROUP = ("yl", "yh", "x", "c")
level_shift = 0.3
DSTEP = 8


def lookup(indices, table):
    choices_range = jnp.arange(table.shape[0], dtype=jnp.int32)
    return jnp.sum(
        jnp.where(indices[:, None] == choices_range[None, :], table[None, :], 0.0), axis=1
    )


def ladder_kernel(
    where_ref, own_ref, other_ref, r0_ref, rp_ref, rm_ref, rt_ref, left_ref, out_ref, bmat, xs, wide, lefts, acc
):
    x, c = where_ref[0], where_ref[1]
    step = pl.program_id(0)

    @pl.when(step == 0)
    def _():
        acc[...] = jnp.zeros_like(acc)
        wide[...] = left_ref[...].astype(jnp.float32)
        for ref, shift in ((r0_ref, 0), (rp_ref, 3), (rm_ref, 1), (rt_ref, 2)):
            source = (x + shift) & 3
            for yh in range(2):
                for yl in range(4):
                    for cc in range(2):
                        for r in range(2):
                            d = pl.multiple_of((yh * 4 + source) * 64 + cc * 32, 32)
                            b = yl * 2 + r
                            bmat[pl.ds(d, 32), b * 128 : (b + 1) * 128] = ref[
                                (yh * 4 + yl) * 2 + cc, r * 32 : r * 32 + 32, :
                            ]

    for dd in range(DSTEP):
        for cc in range(2):
            for r in range(2):
                start = cc * 64 + r * 32 + step * DSTEP + dd
                lefts[dd, r * 32 : (r + 1) * 32, cc * 128 : (cc + 1) * 128] = wide[
                    pl.ds(start, 32, stride=128), :
                ].astype(jnp.bfloat16)

    for amps_ref, cc in ((own_ref, c), (other_ref, 1 - c)):
        amps = amps_ref[...].reshape(DSTEP * 64, 512)
        lanes = pl.ds(pl.multiple_of(cc * 128, 128), 128)
        for bb in range(4):
            prod = jnp.dot(
                amps, bmat[:, bb * 256 : (bb + 1) * 256], preferred_element_type=jnp.float32
            ).astype(jnp.bfloat16)
            for dd in range(DSTEP):
                for r in range(2):
                    b = bb * 2 + r
                    xs[dd, b * 64 : (b + 1) * 64, lanes] = prod[
                        dd * 64 : (dd + 1) * 64, r * 128 : (r + 1) * 128
                    ]
    total = acc[...]
    for dd in range(DSTEP):
        total += lax.dot_general(
            xs[dd], lefts[dd], (((1,), (1,)), ((), ())), preferred_element_type=jnp.float32
        )
    acc[...] = total

    @pl.when(step == pl.num_programs(0) - 1)
    def _():
        for yl in range(4):
            w = acc[yl * 128 : (yl + 1) * 128, :].T
            for r in range(2):
                for z in range(8):
                    out_ref[pl.ds(z * 32 + yl * 8 + r, 4, stride=2), :] = w[
                        r * 32 + z * 4 : r * 32 + z * 4 + 4, :
                    ]


def ladder_parts(where, own, other, rights, left):
    block = pl.BlockSpec((DSTEP, 64, 512), lambda i, w: (i, 0, 0))
    whole = pl.BlockSpec((16, 64, 128), lambda i, w: (0, 0, 0))
    return pl.pallas_call(
        ladder_kernel,
        grid_spec=pltpu.PrefetchScalarGridSpec(
            num_scalar_prefetch=1,
            grid=(32 // DSTEP,),
            in_specs=[block, block, whole, whole, whole, whole]
            + [pl.BlockSpec((4096, 128), lambda i, w: (0, 0))],
            out_specs=pl.BlockSpec((256, 128), lambda i, w: (0, 0)),
            scratch_shapes=[
                pltpu.VMEM((512, 1024), jnp.bfloat16),
                pltpu.VMEM((DSTEP, 512, 256), jnp.bfloat16),
                pltpu.VMEM((4096, 128), jnp.float32),
                pltpu.VMEM((DSTEP, 64, 256), jnp.bfloat16),
                pltpu.VMEM((512, 64), jnp.float32),
            ],
        ),
        out_shape=jax.ShapeDtypeStruct((256, 128), jnp.float32),
        compiler_params=pltpu.CompilerParams(
            dimension_semantics=("arbitrary",), vmem_limit_bytes=58 * 1024 * 1024
        ),
        cost_estimate=pl.CostEstimate(
            flops=2 * 4096 * 512 * 1024 + 2 * 64 * 64 * 8 * 8192,
            bytes_accessed=6 * 1024 * 1024,
            transcendentals=0,
        ),
    )(where, own, other, *rights, left)


def both_kernel(own_ref, crossed_ref, pairing_ref, out_ref, turned):
    for yl in range(4):
        rows = [crossed_ref[pl.ds(yl * 2 + r, 32, stride=8), :] for r in range(2)]
        for r in range(2):
            half = slice(r * 64, (r + 1) * 64)
            turned[pl.ds(r, 32, stride=2), :] = jnp.concatenate(
                [rows[0][:, half], rows[1][:, half]], axis=1
            )
        partnered = jnp.dot(
            turned[...],
            pairing_ref[...],
            precision=lax.Precision.HIGHEST,
            preferred_element_type=jnp.float32,
        )
        for z in range(8):
            total = own_ref[z * 32 + yl * 8 : z * 32 + yl * 8 + 8, :] + partnered[z * 8 : z * 8 + 8]
            out_ref[(yl * 8 + z) * 2] = total[:4]
            out_ref[(yl * 8 + z) * 2 + 1] = total[4:]


def both_orders(own, crossed, pairing):
    return pl.pallas_call(
        both_kernel,
        out_shape=jax.ShapeDtypeStruct((64, 4, 128), jnp.float32),
        scratch_shapes=[pltpu.VMEM((64, 128), jnp.float32)],
    )(own, crossed, pairing)


def finish_kernel(parts_ref, shift_ref, out_ref):
    update = jnp.sum(parts_ref[...], axis=0) / shift_ref[...]
    for r in range(2):
        for i in range(4):
            out_ref[r : r + 1, i * 64 : (i + 1) * 64] = update[i : i + 1, r * 64 : (r + 1) * 64]


def finished(parts, shift):
    return pl.pallas_call(
        finish_kernel, out_shape=jax.ShapeDtypeStruct((2, 256), jnp.float32)
    )(parts, shift)


def per_device(factors, amplitudes, pair_order, occ_bin, vir_bin, levels):
    swapped = pair_order % NOCC * NOCC + pair_order // NOCC
    matches = (pair_order[:, None] == swapped[None, :]).astype(jnp.float32)
    pairing = jnp.kron(jnp.eye(2, dtype=jnp.float32), matches)
    virtual_energy = lookup(vir_bin, levels)
    occupied_energy = -lookup(occ_bin, levels)
    pair_energy = lookup(pair_order // NOCC, occupied_energy) + lookup(
        pair_order % NOCC, occupied_energy
    )
    left_energy = lax.dynamic_slice_in_dim(virtual_energy, lax.axis_index(DEV) * 4, 4)
    right_energy = lax.dynamic_slice_in_dim(virtual_energy, lax.axis_index(BA) * 2, 2)
    denominator = (
        right_energy[None, :, None]
        + left_energy[:, None, None]
        - pair_energy[None, None, :]
        + level_shift
    ).reshape(4, 128)

    eighths = factors.reshape(64, 8, 128).transpose(1, 0, 2)
    eighths = jnp.broadcast_to(eighths[None], (2, 8, 64, 128)).reshape(16, 64, 128)
    rows = lax.all_to_all(eighths, ("yh", "yl", "c"), 0, 0, tiled=True)
    amps = amplitudes.transpose(1, 0, 2)
    rows, sent = lax.optimization_barrier((rows, amps))
    amps_other = lax.ppermute(sent, "c", [(0, 1), (1, 0)])
    own = lax.dynamic_slice_in_dim(rows, lax.axis_index("yh") * 8, 8)
    own = jnp.broadcast_to(own.reshape(1, 512, 128), (8, 512, 128))
    left = lax.all_to_all(own, "z", 0, 0, tiled=True).reshape(4096, 128)
    rights = [rows] + [
        lax.ppermute(rows, "x", [(i, (i + s) % 4) for i in range(4)]) for s in (1, 3, 2)
    ]
    where = jnp.stack([lax.axis_index("x"), lax.axis_index("c")]).astype(jnp.int32)
    ladder = ladder_parts(where, amps, amps_other, rights, left)
    crossed = lax.all_to_all(ladder.reshape(8, 32, 128), "z", 0, 0, tiled=True)
    parts = both_orders(ladder, crossed.reshape(256, 128), pairing)
    parts = lax.all_to_all(parts, GROUP, 0, 0, tiled=True)
    return finished(parts, denominator)


def solution(mesh):
    finer = Mesh(mesh.devices.reshape(SIZES), AXES)
    return jax.shard_map(
        per_device,
        mesh=finer,
        in_specs=(P(BA, DEV, None), P(None, DEV, None), P(), P(), P(), P()),
        out_specs=P(BA, DEV),
        check_vma=False,
    )
```

```python
import functools

import jax
import jax.numpy as jnp
from jax import lax
from jax.experimental import pallas as pl
from jax.experimental.pallas import tpu as pltpu
from jax.sharding import Mesh
from jax.sharding import PartitionSpec as P

NOCC = 8
AXES = ("z", "yl", "yh", "x", "c")
SIZES = (8, 4, 2, 4, 2)
BA = ("z", "yl")
DEV = ("yh", "x", "c")
GROUP = ("yl", "yh", "x", "c")
level_shift = 0.3
DSTEP = 8
VMEM_A = 24
VMEM_B = 54


def lookup(indices, table):
    choices_range = jnp.arange(table.shape[0], dtype=jnp.int32)
    return jnp.sum(
        jnp.where(indices[:, None] == choices_range[None, :], table[None, :], 0.0), axis=1
    )


def product_kernel(where_ref, own_ref, other_ref, r0_ref, rp_ref, rm_ref, rt_ref, out_ref, bmat):
    x, c = where_ref[0], where_ref[1]

    @pl.when(pl.program_id(0) == 0)
    def _():
        for ref, shift in ((r0_ref, 0), (rp_ref, 3), (rm_ref, 1), (rt_ref, 2)):
            source = (x + shift) & 3
            for yh in range(2):
                for yl in range(4):
                    for cc in range(2):
                        for r in range(2):
                            d = pl.multiple_of((yh * 4 + source) * 64 + cc * 32, 32)
                            b = yl * 2 + r
                            bmat[pl.ds(d, 32), b * 128 : (b + 1) * 128] = ref[
                                (yh * 4 + yl) * 2 + cc, r * 32 : r * 32 + 32, :
                            ]

    for amps_ref, cc in ((own_ref, c), (other_ref, 1 - c)):
        amps = amps_ref[...].reshape(DSTEP * 64, 512)
        for bb in range(4):
            prod = jnp.dot(
                amps, bmat[:, bb * 256 : (bb + 1) * 256], preferred_element_type=jnp.float32
            ).astype(jnp.bfloat16)
            for dd in range(DSTEP):
                lanes = pl.ds(pl.multiple_of(dd * 256 + cc * 128, 128), 128)
                for r in range(2):
                    b = bb * 2 + r
                    out_ref[0, b * 64 : (b + 1) * 64, lanes] = prod[
                        dd * 64 : (dd + 1) * 64, r * 128 : (r + 1) * 128
                    ]


def products(where, own, other, rights):
    block = pl.BlockSpec((DSTEP, 64, 512), lambda i, w: (i, 0, 0))
    whole = pl.BlockSpec((16, 64, 128), lambda i, w: (0, 0, 0))
    return pl.pallas_call(
        product_kernel,
        grid_spec=pltpu.PrefetchScalarGridSpec(
            num_scalar_prefetch=1,
            grid=(32 // DSTEP,),
            in_specs=[block, block, whole, whole, whole, whole],
            out_specs=pl.BlockSpec((1, 512, DSTEP * 256), lambda i, w: (i, 0, 0)),
            scratch_shapes=[pltpu.VMEM((512, 1024), jnp.bfloat16)],
        ),
        out_shape=pltpu.HBM((32 // DSTEP, 512, DSTEP * 256), jnp.bfloat16),
        compiler_params=pltpu.CompilerParams(
            dimension_semantics=("arbitrary",), vmem_limit_bytes=VMEM_A * 1024 * 1024
        ),
        cost_estimate=pl.CostEstimate(
            flops=2 * 4096 * 512 * 1024, bytes_accessed=14 * 1024 * 1024, transcendentals=0
        ),
    )(where, own, other, *rights)


def ladder_kernel(prod_ref, left_ref, out_ref, wide, lefts, acc):
    step = pl.program_id(0)

    @pl.when(step == 0)
    def _():
        acc[...] = jnp.zeros_like(acc)
        wide[...] = left_ref[...].astype(jnp.float32)

    for dd in range(DSTEP):
        for cc in range(2):
            lane = dd * 256 + cc * 128
            for r in range(2):
                start = cc * 64 + r * 32 + step * DSTEP + dd
                lefts[r * 32 : (r + 1) * 32, lane : lane + 128] = wide[
                    pl.ds(start, 32, stride=128), :
                ].astype(jnp.bfloat16)
    acc[...] += lax.dot_general(
        lefts[...], prod_ref[0], (((1,), (1,)), ((), ())), preferred_element_type=jnp.float32
    )

    @pl.when(step == pl.num_programs(0) - 1)
    def _():
        for yl in range(4):
            for r in range(2):
                for z in range(8):
                    out_ref[pl.ds(z * 32 + yl * 8 + r, 4, stride=2), :] = acc[
                        r * 32 + z * 4 : r * 32 + z * 4 + 4, yl * 128 : (yl + 1) * 128
                    ]


def ladder_parts(prods, left):
    return pl.pallas_call(
        ladder_kernel,
        grid=(32 // DSTEP,),
        in_specs=[
            pl.BlockSpec((1, 512, DSTEP * 256), lambda i: (i, 0, 0)),
            pl.BlockSpec((4096, 128), lambda i: (0, 0)),
        ],
        out_specs=pl.BlockSpec((256, 128), lambda i: (0, 0)),
        out_shape=jax.ShapeDtypeStruct((256, 128), jnp.float32),
        scratch_shapes=[
            pltpu.VMEM((4096, 128), jnp.float32),
            pltpu.VMEM((64, DSTEP * 256), jnp.bfloat16),
            pltpu.VMEM((64, 512), jnp.float32),
        ],
        compiler_params=pltpu.CompilerParams(
            dimension_semantics=("arbitrary",), vmem_limit_bytes=VMEM_B * 1024 * 1024
        ),
        cost_estimate=pl.CostEstimate(
            flops=2 * 64 * 64 * 8 * 8192, bytes_accessed=9 * 1024 * 1024, transcendentals=0
        ),
    )(prods, left)


def both_kernel(own_ref, crossed_ref, pairing_ref, out_ref, turned):
    for yl in range(4):
        rows = [crossed_ref[pl.ds(yl * 2 + r, 32, stride=8), :] for r in range(2)]
        for r in range(2):
            half = slice(r * 64, (r + 1) * 64)
            turned[pl.ds(r, 32, stride=2), :] = jnp.concatenate(
                [rows[0][:, half], rows[1][:, half]], axis=1
            )
        partnered = jnp.dot(
            turned[...],
            pairing_ref[...],
            precision=lax.Precision.HIGHEST,
            preferred_element_type=jnp.float32,
        )
        for z in range(8):
            total = own_ref[z * 32 + yl * 8 : z * 32 + yl * 8 + 8, :] + partnered[z * 8 : z * 8 + 8]
            out_ref[(yl * 8 + z) * 2] = total[:4]
            out_ref[(yl * 8 + z) * 2 + 1] = total[4:]


def both_orders(own, crossed, pairing):
    return pl.pallas_call(
        both_kernel,
        out_shape=jax.ShapeDtypeStruct((64, 4, 128), jnp.float32),
        scratch_shapes=[pltpu.VMEM((64, 128), jnp.float32)],
        compiler_params=pltpu.CompilerParams(vmem_limit_bytes=8 * 1024 * 1024),
    )(own, crossed, pairing)


def finish_kernel(parts_ref, shift_ref, out_ref):
    update = jnp.sum(parts_ref[...], axis=0) / shift_ref[...]
    for r in range(2):
        for i in range(4):
            out_ref[r : r + 1, i * 64 : (i + 1) * 64] = update[i : i + 1, r * 64 : (r + 1) * 64]


def finished(parts, shift):
    return pl.pallas_call(
        finish_kernel,
        out_shape=jax.ShapeDtypeStruct((2, 256), jnp.float32),
        compiler_params=pltpu.CompilerParams(vmem_limit_bytes=8 * 1024 * 1024),
    )(parts, shift)


def per_device(factors, amplitudes, pair_order, occ_bin, vir_bin, levels):
    swapped = pair_order % NOCC * NOCC + pair_order // NOCC
    matches = (pair_order[:, None] == swapped[None, :]).astype(jnp.float32)
    pairing = jnp.kron(jnp.eye(2, dtype=jnp.float32), matches)
    virtual_energy = lookup(vir_bin, levels)
    occupied_energy = -lookup(occ_bin, levels)
    pair_energy = lookup(pair_order // NOCC, occupied_energy) + lookup(
        pair_order % NOCC, occupied_energy
    )
    left_energy = lax.dynamic_slice_in_dim(virtual_energy, lax.axis_index(DEV) * 4, 4)
    right_energy = lax.dynamic_slice_in_dim(virtual_energy, lax.axis_index(BA) * 2, 2)
    denominator = (
        right_energy[None, :, None]
        + left_energy[:, None, None]
        - pair_energy[None, None, :]
        + level_shift
    ).reshape(4, 128)

    eighths = factors.reshape(64, 8, 128).transpose(1, 0, 2)
    eighths = jnp.broadcast_to(eighths[None], (2, 8, 64, 128)).reshape(16, 64, 128)
    rows = lax.all_to_all(eighths, ("yh", "yl", "c"), 0, 0, tiled=True)
    amps = amplitudes.transpose(1, 0, 2)
    rows, sent = lax.optimization_barrier((rows, amps))
    amps_other = lax.ppermute(sent, "c", [(0, 1), (1, 0)])
    own = lax.dynamic_slice_in_dim(rows, lax.axis_index("yh") * 8, 8)
    own = jnp.broadcast_to(own.reshape(1, 512, 128), (8, 512, 128))
    left = lax.all_to_all(own, "z", 0, 0, tiled=True).reshape(4096, 128)
    rights = [rows] + [
        lax.ppermute(rows, "x", [(i, (i + s) % 4) for i in range(4)]) for s in (1, 3, 2)
    ]
    where = jnp.stack([lax.axis_index("x"), lax.axis_index("c")]).astype(jnp.int32)
    ladder = ladder_parts(products(where, amps, amps_other, rights), left)
    crossed = lax.all_to_all(ladder.reshape(8, 32, 128), "z", 0, 0, tiled=True)
    parts = both_orders(ladder, crossed.reshape(256, 128), pairing)
    parts = lax.all_to_all(parts, GROUP, 0, 0, tiled=True)
    return finished(parts, denominator)


def solution(mesh):
    finer = Mesh(mesh.devices.reshape(SIZES), AXES)
    return jax.shard_map(
        per_device,
        mesh=finer,
        in_specs=(P(BA, DEV, None), P(None, DEV, None), P(), P(), P(), P()),
        out_specs=P(BA, DEV),
        check_vma=False,
    )
```

```python
import functools

import jax
import jax.numpy as jnp
from jax import lax
from jax.experimental import pallas as pl
from jax.experimental.pallas import tpu as pltpu
from jax.sharding import Mesh
from jax.sharding import PartitionSpec as P

NOCC = 8
AXES = ("z", "yl", "yh", "x", "c")
SIZES = (8, 4, 2, 4, 2)
BA = ("z", "yl")
DEV = ("yh", "x", "c")
GROUP = ("yl", "yh", "x", "c")
level_shift = 0.3
DSTEP = 8
STEPS = 4
VMEM_A = 24
VMEM_B = 49


def lookup(indices, table):
    choices_range = jnp.arange(table.shape[0], dtype=jnp.int32)
    return jnp.sum(
        jnp.where(indices[:, None] == choices_range[None, :], table[None, :], 0.0), axis=1
    )


def product_kernel(
    where_ref, own_ref, other_ref, r0_ref, rp_ref, rm_ref, rt_ref, out_ref, amps, bmat, prods, amps_sem, b_sem, out_sem
):
    x, c = where_ref[0], where_ref[1]
    rights = [
        pltpu.make_async_copy(ref, bmat.at[(x + shift) & 3], b_sem.at[n])
        for n, (ref, shift) in enumerate(((r0_ref, 0), (rp_ref, 3), (rm_ref, 1), (rt_ref, 2)))
    ]

    def load(step, half):
        ref, place = ((own_ref, c), (other_ref, 1 - c))[half]
        return pltpu.make_async_copy(ref.at[step], amps.at[place, step], amps_sem.at[half, step])

    def store(step):
        return pltpu.make_async_copy(prods.at[step], out_ref.at[step], out_sem.at[step])

    for copy in rights:
        copy.start()
    for step in range(STEPS):
        load(step, 0).start()
        load(step, 1).start()
    for copy in rights:
        copy.wait()

    def one_step(step, _):
        load(step, 0).wait()
        load(step, 1).wait()
        for yl in range(4):
            right = jnp.concatenate(
                [
                    jnp.concatenate(
                        [bmat[x, (yh * 4 + yl) * 2 + cc, r * 32 : r * 32 + 32, :] for r in range(2)],
                        axis=1,
                    )
                    for yh in range(2)
                    for x in range(4)
                    for cc in range(2)
                ],
                axis=0,
            )
            for cc in range(2):
                prod = jnp.dot(
                    amps[cc, step].reshape(DSTEP * 64, 512), right, preferred_element_type=jnp.float32
                ).astype(jnp.bfloat16)
                for dd in range(DSTEP):
                    lane = dd * 256 + cc * 128
                    for r in range(2):
                        b = yl * 2 + r
                        prods[step, b * 64 : (b + 1) * 64, lane : lane + 128] = prod[
                            dd * 64 : (dd + 1) * 64, r * 128 : (r + 1) * 128
                        ]
        store(step).start()
        return 0

    lax.fori_loop(0, STEPS, one_step, 0)
    for step in range(STEPS):
        store(step).wait()


def products(where, own, other, rights):
    anywhere = pl.BlockSpec(memory_space=pl.ANY)
    shape = (STEPS, 512, DSTEP * 256)
    return pl.pallas_call(
        product_kernel,
        in_specs=[pl.BlockSpec(memory_space=pltpu.SMEM)] + [anywhere] * 6,
        out_specs=pl.BlockSpec(memory_space=pltpu.HBM),
        out_shape=pltpu.HBM(shape, jnp.bfloat16),
        scratch_shapes=[
            pltpu.VMEM((2, STEPS, DSTEP, 64, 512), jnp.bfloat16),
            pltpu.VMEM((4, 16, 64, 128), jnp.bfloat16),
            pltpu.VMEM(shape, jnp.bfloat16),
            pltpu.SemaphoreType.DMA((2, STEPS)),
            pltpu.SemaphoreType.DMA((4,)),
            pltpu.SemaphoreType.DMA((STEPS,)),
        ],
        compiler_params=pltpu.CompilerParams(vmem_limit_bytes=VMEM_A * 1024 * 1024),
        cost_estimate=pl.CostEstimate(
            flops=2 * 4096 * 512 * 1024, bytes_accessed=14 * 1024 * 1024, transcendentals=0
        ),
    )(where, own, other, *rights)


def ladder_kernel(prod_ref, left_ref, out_ref, prods, wide, lefts, sem):
    copies = [
        pltpu.make_async_copy(prod_ref.at[step], prods.at[step], sem.at[step])
        for step in range(STEPS)
    ]
    for copy in copies:
        copy.start()
    wide[...] = left_ref[...].astype(jnp.float32)
    for step in range(STEPS):
        for dd in range(DSTEP):
            for cc in range(2):
                lane = dd * 256 + cc * 128
                for r in range(2):
                    start = cc * 64 + r * 32 + step * DSTEP + dd
                    lefts[step, r * 32 : (r + 1) * 32, lane : lane + 128] = wide[
                        pl.ds(start, 32, stride=128), :
                    ].astype(jnp.bfloat16)
    total = jnp.zeros((64, 512), jnp.float32)
    for step in range(STEPS):
        copies[step].wait()
        total += lax.dot_general(
            lefts[step], prods[step], (((1,), (1,)), ((), ())), preferred_element_type=jnp.float32
        )
    for yl in range(4):
        for r in range(2):
            for z in range(8):
                out_ref[pl.ds(z * 32 + yl * 8 + r, 4, stride=2), :] = total[
                    r * 32 + z * 4 : r * 32 + z * 4 + 4, yl * 128 : (yl + 1) * 128
                ]


def ladder_parts(prods, left):
    return pl.pallas_call(
        ladder_kernel,
        in_specs=[
            pl.BlockSpec(memory_space=pltpu.HBM),
            pl.BlockSpec(memory_space=pltpu.VMEM),
        ],
        out_specs=pl.BlockSpec(memory_space=pltpu.VMEM),
        out_shape=jax.ShapeDtypeStruct((256, 128), jnp.float32),
        scratch_shapes=[
            pltpu.VMEM((STEPS, 512, DSTEP * 256), jnp.bfloat16),
            pltpu.VMEM((4096, 128), jnp.float32),
            pltpu.VMEM((STEPS, 64, DSTEP * 256), jnp.bfloat16),
            pltpu.SemaphoreType.DMA((STEPS,)),
        ],
        compiler_params=pltpu.CompilerParams(vmem_limit_bytes=VMEM_B * 1024 * 1024),
        cost_estimate=pl.CostEstimate(
            flops=2 * 64 * 64 * 8 * 8192, bytes_accessed=9 * 1024 * 1024, transcendentals=0
        ),
    )(prods, left)


def both_kernel(own_ref, crossed_ref, pairing_ref, out_ref, turned):
    for yl in range(4):
        rows = [crossed_ref[pl.ds(yl * 2 + r, 32, stride=8), :] for r in range(2)]
        for r in range(2):
            half = slice(r * 64, (r + 1) * 64)
            turned[pl.ds(r, 32, stride=2), :] = jnp.concatenate(
                [rows[0][:, half], rows[1][:, half]], axis=1
            )
        partnered = jnp.dot(
            turned[...],
            pairing_ref[...],
            precision=lax.Precision.HIGHEST,
            preferred_element_type=jnp.float32,
        )
        for z in range(8):
            total = own_ref[z * 32 + yl * 8 : z * 32 + yl * 8 + 8, :] + partnered[z * 8 : z * 8 + 8]
            out_ref[(yl * 8 + z) * 2] = total[:4]
            out_ref[(yl * 8 + z) * 2 + 1] = total[4:]


def both_orders(own, crossed, pairing):
    return pl.pallas_call(
        both_kernel,
        out_shape=jax.ShapeDtypeStruct((64, 4, 128), jnp.float32),
        scratch_shapes=[pltpu.VMEM((64, 128), jnp.float32)],
        compiler_params=pltpu.CompilerParams(vmem_limit_bytes=8 * 1024 * 1024),
    )(own, crossed, pairing)


def finish_kernel(parts_ref, shift_ref, out_ref):
    update = jnp.sum(parts_ref[...], axis=0) / shift_ref[...]
    for r in range(2):
        for i in range(4):
            out_ref[r : r + 1, i * 64 : (i + 1) * 64] = update[i : i + 1, r * 64 : (r + 1) * 64]


def finished(parts, shift):
    return pl.pallas_call(
        finish_kernel,
        out_shape=jax.ShapeDtypeStruct((2, 256), jnp.float32),
        compiler_params=pltpu.CompilerParams(vmem_limit_bytes=8 * 1024 * 1024),
    )(parts, shift)


def per_device(factors, amplitudes, pair_order, occ_bin, vir_bin, levels):
    swapped = pair_order % NOCC * NOCC + pair_order // NOCC
    matches = (pair_order[:, None] == swapped[None, :]).astype(jnp.float32)
    pairing = jnp.kron(jnp.eye(2, dtype=jnp.float32), matches)
    virtual_energy = lookup(vir_bin, levels)
    occupied_energy = -lookup(occ_bin, levels)
    pair_energy = lookup(pair_order // NOCC, occupied_energy) + lookup(
        pair_order % NOCC, occupied_energy
    )
    left_energy = lax.dynamic_slice_in_dim(virtual_energy, lax.axis_index(DEV) * 4, 4)
    right_energy = lax.dynamic_slice_in_dim(virtual_energy, lax.axis_index(BA) * 2, 2)
    denominator = (
        right_energy[None, :, None]
        + left_energy[:, None, None]
        - pair_energy[None, None, :]
        + level_shift
    ).reshape(4, 128)

    eighths = factors.reshape(64, 8, 128).transpose(1, 0, 2)
    eighths = jnp.broadcast_to(eighths[None], (2, 8, 64, 128)).reshape(16, 64, 128)
    rows = lax.all_to_all(eighths, ("yh", "yl", "c"), 0, 0, tiled=True)
    other = lax.ppermute(amplitudes, "c", [(0, 1), (1, 0)])
    amps, amps_other = (
        t.transpose(1, 0, 2).reshape(STEPS, DSTEP, 64, 512) for t in (amplitudes, other)
    )
    own = lax.dynamic_slice_in_dim(rows, lax.axis_index("yh") * 8, 8)
    own = jnp.broadcast_to(own.reshape(1, 512, 128), (8, 512, 128))
    left = lax.all_to_all(own, "z", 0, 0, tiled=True).reshape(4096, 128)
    rights = [rows] + [
        lax.ppermute(rows, "x", [(i, (i + s) % 4) for i in range(4)]) for s in (1, 3, 2)
    ]
    where = jnp.stack([lax.axis_index("x"), lax.axis_index("c")]).astype(jnp.int32)
    ladder = ladder_parts(products(where, amps, amps_other, rights), left)
    crossed = lax.all_to_all(ladder.reshape(8, 32, 128), "z", 0, 0, tiled=True)
    parts = both_orders(ladder, crossed.reshape(256, 128), pairing)
    parts = lax.all_to_all(parts, GROUP, 0, 0, tiled=True)
    return finished(parts, denominator)


def solution(mesh):
    finer = Mesh(mesh.devices.reshape(SIZES), AXES)
    return jax.shard_map(
        per_device,
        mesh=finer,
        in_specs=(P(BA, DEV, None), P(None, DEV, None), P(), P(), P(), P()),
        out_specs=P(BA, DEV),
        check_vma=False,
    )
```

```python
import functools

import jax
import jax.numpy as jnp
from jax import lax
from jax.experimental import pallas as pl
from jax.experimental.pallas import tpu as pltpu
from jax.sharding import Mesh
from jax.sharding import PartitionSpec as P

NOCC = 8
AXES = ("z", "yl", "yh", "x", "c")
SIZES = (8, 4, 2, 4, 2)
BA = ("z", "yl")
DEV = ("yh", "x", "c")
GROUP = ("yh", "x", "yl", "c")
level_shift = 0.3
DSTEP = 8
STEPS = 4
VMEM_A = 24
VMEM_B = 49


def lookup(indices, table):
    choices_range = jnp.arange(table.shape[0], dtype=jnp.int32)
    return jnp.sum(
        jnp.where(indices[:, None] == choices_range[None, :], table[None, :], 0.0), axis=1
    )


def product_kernel(
    where_ref, own_ref, other_ref, r0_ref, rt_ref, rp_ref, rm_ref, out_ref, amps, bmat, prods, amps_sem, b_sem, out_sem
):
    x, c = where_ref[0], where_ref[1]
    rights = [
        pltpu.make_async_copy(ref, bmat.at[(x + shift) & 3], b_sem.at[n])
        for n, (ref, shift) in enumerate(((r0_ref, 0), (rt_ref, 2), (rp_ref, 3), (rm_ref, 1)))
    ]

    def load(step, half):
        ref, place = ((own_ref, c), (other_ref, 1 - c))[half]
        return pltpu.make_async_copy(ref.at[step], amps.at[place, step], amps_sem.at[half, step])

    def store(step):
        return pltpu.make_async_copy(prods.at[step], out_ref.at[step], out_sem.at[step])

    for copy in rights:
        copy.start()
    for step in range(STEPS):
        load(step, 0).start()
        load(step, 1).start()
    for copy in rights:
        copy.wait()

    def one_step(step, _):
        load(step, 0).wait()
        load(step, 1).wait()
        for yl in range(4):
            right = jnp.concatenate(
                [
                    jnp.concatenate(
                        [bmat[x, (yh * 4 + yl) * 2 + cc, r * 32 : r * 32 + 32, :] for r in range(2)],
                        axis=1,
                    )
                    for yh in range(2)
                    for x in range(4)
                    for cc in range(2)
                ],
                axis=0,
            )
            for cc in range(2):
                prod = jnp.dot(
                    amps[cc, step].reshape(DSTEP * 64, 512), right, preferred_element_type=jnp.float32
                ).astype(jnp.bfloat16)
                for dd in range(DSTEP):
                    lane = dd * 256 + cc * 128
                    for r in range(2):
                        b = yl * 2 + r
                        prods[step, b * 64 : (b + 1) * 64, lane : lane + 128] = prod[
                            dd * 64 : (dd + 1) * 64, r * 128 : (r + 1) * 128
                        ]
        store(step).start()
        return 0

    lax.fori_loop(0, STEPS, one_step, 0)
    for step in range(STEPS):
        store(step).wait()


def products(where, own, other, rights):
    anywhere = pl.BlockSpec(memory_space=pl.ANY)
    shape = (STEPS, 512, DSTEP * 256)
    return pl.pallas_call(
        product_kernel,
        in_specs=[pl.BlockSpec(memory_space=pltpu.SMEM)] + [anywhere] * 6,
        out_specs=pl.BlockSpec(memory_space=pltpu.HBM),
        out_shape=pltpu.HBM(shape, jnp.bfloat16),
        scratch_shapes=[
            pltpu.VMEM((2, STEPS, DSTEP, 64, 512), jnp.bfloat16),
            pltpu.VMEM((4, 16, 64, 128), jnp.bfloat16),
            pltpu.VMEM(shape, jnp.bfloat16),
            pltpu.SemaphoreType.DMA((2, STEPS)),
            pltpu.SemaphoreType.DMA((4,)),
            pltpu.SemaphoreType.DMA((STEPS,)),
        ],
        compiler_params=pltpu.CompilerParams(vmem_limit_bytes=VMEM_A * 1024 * 1024),
        cost_estimate=pl.CostEstimate(
            flops=2 * 4096 * 512 * 1024, bytes_accessed=14 * 1024 * 1024, transcendentals=0
        ),
    )(where, own, other, *rights)


def ladder_kernel(prod_ref, left_ref, pairing_ref, own_ref, sent_ref, prods, wide, lefts, sem):
    copies = [
        pltpu.make_async_copy(prod_ref.at[step], prods.at[step], sem.at[step])
        for step in range(STEPS)
    ]
    for copy in copies:
        copy.start()
    wide[...] = left_ref[...].astype(jnp.float32)
    total = jnp.zeros((64, 512), jnp.float32)
    for step in range(STEPS):
        for dd in range(DSTEP):
            for cc in range(2):
                lane = dd * 256 + cc * 128
                for r in range(2):
                    start = cc * 64 + r * 32 + step * DSTEP + dd
                    lefts[step, r * 32 : (r + 1) * 32, lane : lane + 128] = wide[
                        pl.ds(start, 32, stride=128), :
                    ].astype(jnp.bfloat16)
        copies[step].wait()
        total += lax.dot_general(
            lefts[step], prods[step], (((1,), (1,)), ((), ())), preferred_element_type=jnp.float32
        )
    for yl in range(4):
        rows = total[:, yl * 128 : (yl + 1) * 128]
        for r in range(2):
            for z in range(8):
                own_ref[pl.ds(z * 32 + yl * 8 + r, 4, stride=2), :] = rows[
                    r * 32 + z * 4 : r * 32 + z * 4 + 4, :
                ]
        rows = jnp.dot(
            rows,
            pairing_ref[...],
            precision=lax.Precision.HIGHEST,
            preferred_element_type=jnp.float32,
        )
        for r in range(2):
            sent_ref[pl.ds(yl * 2 + r, 32, stride=8), :] = jnp.concatenate(
                [rows[:32, r * 64 : (r + 1) * 64], rows[32:, r * 64 : (r + 1) * 64]], axis=1
            )


def ladder_parts(prods, left, pairing):
    inside = pl.BlockSpec(memory_space=pltpu.VMEM)
    return pl.pallas_call(
        ladder_kernel,
        in_specs=[pl.BlockSpec(memory_space=pltpu.HBM), inside, inside],
        out_specs=[inside] * 2,
        out_shape=[jax.ShapeDtypeStruct((256, 128), jnp.float32)] * 2,
        scratch_shapes=[
            pltpu.VMEM((STEPS, 512, DSTEP * 256), jnp.bfloat16),
            pltpu.VMEM((4096, 128), jnp.float32),
            pltpu.VMEM((STEPS, 64, DSTEP * 256), jnp.bfloat16),
            pltpu.SemaphoreType.DMA((STEPS,)),
        ],
        compiler_params=pltpu.CompilerParams(vmem_limit_bytes=VMEM_B * 1024 * 1024),
        cost_estimate=pl.CostEstimate(
            flops=2 * 64 * 64 * 8 * 8192, bytes_accessed=9 * 1024 * 1024, transcendentals=0
        ),
    )(prods, left, pairing)


def finish_kernel(parts_ref, shift_ref, out_ref):
    update = jnp.sum(parts_ref[...], axis=0) / shift_ref[...]
    for r in range(2):
        for i in range(4):
            out_ref[r : r + 1, i * 64 : (i + 1) * 64] = update[i : i + 1, r * 64 : (r + 1) * 64]


def finished(parts, shift):
    return pl.pallas_call(
        finish_kernel,
        out_shape=jax.ShapeDtypeStruct((2, 256), jnp.float32),
        compiler_params=pltpu.CompilerParams(vmem_limit_bytes=8 * 1024 * 1024),
    )(parts, shift)


def per_device(factors, amplitudes, pair_order, occ_bin, vir_bin, levels):
    swapped = pair_order % NOCC * NOCC + pair_order // NOCC
    matches = (pair_order[:, None] == swapped[None, :]).astype(jnp.float32)
    pairing = jnp.kron(jnp.eye(2, dtype=jnp.float32), matches)
    virtual_energy = lookup(vir_bin, levels)
    occupied_energy = -lookup(occ_bin, levels)
    pair_energy = lookup(pair_order // NOCC, occupied_energy) + lookup(
        pair_order % NOCC, occupied_energy
    )
    left_energy = lax.dynamic_slice_in_dim(virtual_energy, lax.axis_index(DEV) * 4, 4)
    right_energy = lax.dynamic_slice_in_dim(virtual_energy, lax.axis_index(BA) * 2, 2)
    denominator = (
        right_energy[None, :, None]
        + left_energy[:, None, None]
        - pair_energy[None, None, :]
        + level_shift
    ).reshape(4, 128)

    eighths = factors.reshape(64, 8, 128).transpose(1, 0, 2)
    eighths = jnp.broadcast_to(eighths[None], (2, 8, 64, 128)).reshape(16, 64, 128)
    eighths, sent = lax.optimization_barrier((eighths, amplitudes))
    rows = lax.all_to_all(eighths, ("yh", "yl", "c"), 0, 0, tiled=True)
    other = lax.ppermute(sent, "c", [(0, 1), (1, 0)])
    amps, amps_other = (
        t.transpose(1, 0, 2).reshape(STEPS, DSTEP, 64, 512) for t in (amplitudes, other)
    )
    own = lax.dynamic_slice_in_dim(rows, lax.axis_index("yh") * 8, 8)
    own = jnp.broadcast_to(own.reshape(1, 512, 128), (8, 512, 128))
    left = lax.all_to_all(own, "z", 0, 0, tiled=True).reshape(4096, 128)
    rights = [rows] + [
        lax.ppermute(rows, "x", [(i, (i + s) % 4) for i in range(4)]) for s in (2, 1, 3)
    ]
    where = jnp.stack([lax.axis_index("x"), lax.axis_index("c")]).astype(jnp.int32)
    own, sent = ladder_parts(products(where, amps, amps_other, rights), left, pairing)
    crossed = lax.all_to_all(sent.reshape(8, 32, 128), "z", 0, 0, tiled=True)
    parts = (own.reshape(8, 32, 128) + crossed).reshape(64, 4, 128)
    parts = lax.all_to_all(parts, GROUP, 0, 0, tiled=True)
    return finished(parts, denominator)


def solution(mesh):
    finer = Mesh(mesh.devices.reshape(SIZES), AXES)
    return jax.shard_map(
        per_device,
        mesh=finer,
        in_specs=(P(BA, DEV, None), P(None, DEV, None), P(), P(), P(), P()),
        out_specs=P(BA, DEV),
        check_vma=False,
    )
```

```python
import functools

import jax
import jax.numpy as jnp
from jax import lax
from jax.experimental import pallas as pl
from jax.experimental.pallas import tpu as pltpu
from jax.sharding import Mesh
from jax.sharding import PartitionSpec as P

NOCC = 8
AXES = ("z", "yl", "yh", "x", "c")
SIZES = (8, 4, 2, 4, 2)
BA = ("z", "yl")
DEV = ("yh", "x", "c")
GROUP = ("yh", "x", "yl", "c")
level_shift = 0.3
DSTEP = 8
STEPS = 4
VMEM_A = 52
VMEM_B = 49


def lookup(indices, table):
    choices_range = jnp.arange(table.shape[0], dtype=jnp.int32)
    return jnp.sum(
        jnp.where(indices[:, None] == choices_range[None, :], table[None, :], 0.0), axis=1
    )


def product_kernel(
    where_ref, own_ref, other_ref, r0_ref, rt_ref, rp_ref, rm_ref, out_ref, amps, bmat, prods, amps_sem, b_sem, out_sem
):
    x, c = where_ref[0], where_ref[1]
    rights = [
        pltpu.make_async_copy(ref, bmat.at[(x + shift) & 3], b_sem.at[n])
        for n, (ref, shift) in enumerate(((r0_ref, 0), (rt_ref, 2), (rp_ref, 3), (rm_ref, 1)))
    ]

    def load(step, half):
        ref, place = ((own_ref, c), (other_ref, 1 - c))[half]
        return pltpu.make_async_copy(ref.at[step], amps.at[place, step], amps_sem.at[half, step])

    def store(step):
        return pltpu.make_async_copy(prods.at[step], out_ref.at[step], out_sem.at[step])

    for copy in rights:
        copy.start()
    for step in range(STEPS):
        load(step, 0).start()
        load(step, 1).start()
    for copy in rights:
        copy.wait()

    def one_step(step, _):
        load(step, 0).wait()
        load(step, 1).wait()
        for yl in range(4):
            right = jnp.concatenate(
                [
                    jnp.concatenate(
                        [bmat[x, (yh * 4 + yl) * 2 + cc, r * 32 : r * 32 + 32, :] for r in range(2)],
                        axis=1,
                    )
                    for yh in range(2)
                    for x in range(4)
                    for cc in range(2)
                ],
                axis=0,
            )
            for cc in range(2):
                prod = jnp.dot(
                    amps[cc, step].reshape(DSTEP * 64, 512), right, preferred_element_type=jnp.float32
                ).astype(jnp.bfloat16)
                for dd in range(DSTEP):
                    lane = dd * 256 + cc * 128
                    for r in range(2):
                        b = yl * 2 + r
                        prods[step, b * 64 : (b + 1) * 64, lane : lane + 128] = prod[
                            dd * 64 : (dd + 1) * 64, r * 128 : (r + 1) * 128
                        ]
        store(step).start()
        return 0

    lax.fori_loop(0, STEPS, one_step, 0)
    for step in range(STEPS):
        store(step).wait()


def products(where, own, other, rights):
    anywhere = pl.BlockSpec(memory_space=pl.ANY)
    shape = (STEPS, 512, DSTEP * 256)
    return pl.pallas_call(
        product_kernel,
        in_specs=[pl.BlockSpec(memory_space=pltpu.SMEM)] + [anywhere] * 6,
        out_specs=pl.BlockSpec(memory_space=pltpu.HBM),
        out_shape=pltpu.HBM(shape, jnp.bfloat16),
        scratch_shapes=[
            pltpu.VMEM((2, STEPS, DSTEP, 64, 512), jnp.bfloat16),
            pltpu.VMEM((4, 16, 64, 128), jnp.bfloat16),
            pltpu.VMEM(shape, jnp.bfloat16),
            pltpu.SemaphoreType.DMA((2, STEPS)),
            pltpu.SemaphoreType.DMA((4,)),
            pltpu.SemaphoreType.DMA((STEPS,)),
        ],
        compiler_params=pltpu.CompilerParams(vmem_limit_bytes=VMEM_A * 1024 * 1024),
        cost_estimate=pl.CostEstimate(
            flops=2 * 4096 * 512 * 1024, bytes_accessed=14 * 1024 * 1024, transcendentals=0
        ),
    )(where, own, other, *rights)


def ladder_kernel(prod_ref, left_ref, pairing_ref, own_ref, sent_ref, prods, wide, lefts, sem):
    copies = [
        pltpu.make_async_copy(prod_ref.at[step], prods.at[step], sem.at[step])
        for step in range(STEPS)
    ]
    for copy in copies:
        copy.start()
    wide[...] = left_ref[...].astype(jnp.float32)
    total = jnp.zeros((64, 512), jnp.float32)
    for step in range(STEPS):
        for dd in range(DSTEP):
            for cc in range(2):
                lane = dd * 256 + cc * 128
                for r in range(2):
                    start = cc * 64 + r * 32 + step * DSTEP + dd
                    lefts[step, r * 32 : (r + 1) * 32, lane : lane + 128] = wide[
                        pl.ds(start, 32, stride=128), :
                    ].astype(jnp.bfloat16)
        copies[step].wait()
        total += lax.dot_general(
            lefts[step], prods[step], (((1,), (1,)), ((), ())), preferred_element_type=jnp.float32
        )
    chunks = [total[:, yl * 128 : (yl + 1) * 128] for yl in range(4)]
    for yl, rows in enumerate(chunks):
        for r in range(2):
            for z in range(8):
                own_ref[pl.ds(z * 32 + yl * 8 + r, 4, stride=2), :] = rows[
                    r * 32 + z * 4 : r * 32 + z * 4 + 4, :
                ]
    rest = jnp.concatenate(chunks, axis=0)
    paired = jnp.zeros((256, 128), jnp.float32)
    for _ in range(3):
        part = rest.astype(jnp.bfloat16)
        paired += jnp.dot(part, pairing_ref[...], preferred_element_type=jnp.float32)
        rest = rest - part.astype(jnp.float32)
    for yl in range(4):
        rows = paired[yl * 64 : (yl + 1) * 64]
        for r in range(2):
            sent_ref[pl.ds(yl * 2 + r, 32, stride=8), :] = jnp.concatenate(
                [rows[:32, r * 64 : (r + 1) * 64], rows[32:, r * 64 : (r + 1) * 64]], axis=1
            )


def ladder_parts(prods, left, pairing):
    inside = pl.BlockSpec(memory_space=pltpu.VMEM)
    return pl.pallas_call(
        ladder_kernel,
        in_specs=[pl.BlockSpec(memory_space=pltpu.HBM), inside, inside],
        out_specs=[inside] * 2,
        out_shape=[jax.ShapeDtypeStruct((256, 128), jnp.float32)] * 2,
        scratch_shapes=[
            pltpu.VMEM((STEPS, 512, DSTEP * 256), jnp.bfloat16),
            pltpu.VMEM((4096, 128), jnp.float32),
            pltpu.VMEM((STEPS, 64, DSTEP * 256), jnp.bfloat16),
            pltpu.SemaphoreType.DMA((STEPS,)),
        ],
        compiler_params=pltpu.CompilerParams(vmem_limit_bytes=VMEM_B * 1024 * 1024),
        cost_estimate=pl.CostEstimate(
            flops=2 * 64 * 64 * 8 * 8192, bytes_accessed=9 * 1024 * 1024, transcendentals=0
        ),
    )(prods, left, pairing)


def finish_kernel(parts_ref, shift_ref, out_ref):
    update = jnp.sum(parts_ref[...], axis=0) / shift_ref[...]
    for r in range(2):
        for i in range(4):
            out_ref[r : r + 1, i * 64 : (i + 1) * 64] = update[i : i + 1, r * 64 : (r + 1) * 64]


def finished(parts, shift):
    return pl.pallas_call(
        finish_kernel,
        out_shape=jax.ShapeDtypeStruct((2, 256), jnp.float32),
        compiler_params=pltpu.CompilerParams(vmem_limit_bytes=8 * 1024 * 1024),
    )(parts, shift)


def per_device(factors, amplitudes, pair_order, occ_bin, vir_bin, levels):
    swapped = pair_order % NOCC * NOCC + pair_order // NOCC
    lane = jnp.arange(128, dtype=jnp.int32)
    matches = jnp.tile(pair_order, 2)[:, None] == jnp.tile(swapped, 2)[None, :]
    pairing = (matches & (lane[:, None] // 64 == lane[None, :] // 64)).astype(jnp.bfloat16)
    virtual_energy = lookup(vir_bin, levels)
    occupied_energy = -lookup(occ_bin, levels)
    pair_energy = lookup(pair_order // NOCC, occupied_energy) + lookup(
        pair_order % NOCC, occupied_energy
    )
    left_energy = lax.dynamic_slice_in_dim(virtual_energy, lax.axis_index(DEV) * 4, 4)
    right_energy = lax.dynamic_slice_in_dim(virtual_energy, lax.axis_index(BA) * 2, 2)
    denominator = (
        right_energy[None, :, None]
        + left_energy[:, None, None]
        - pair_energy[None, None, :]
        + level_shift
    ).reshape(4, 128)

    eighths = factors.reshape(64, 8, 128).transpose(1, 0, 2)
    eighths = jnp.broadcast_to(eighths[None], (2, 8, 64, 128)).reshape(16, 64, 128)
    eighths, sent = lax.optimization_barrier((eighths, amplitudes))
    rows = lax.all_to_all(eighths, ("yh", "yl", "c"), 0, 0, tiled=True)
    other = lax.ppermute(sent, "c", [(0, 1), (1, 0)])
    amps, amps_other = (
        t.transpose(1, 0, 2).reshape(STEPS, DSTEP, 64, 512) for t in (amplitudes, other)
    )
    rows, amps, amps_other, pairing = lax.optimization_barrier((rows, amps, amps_other, pairing))
    own = lax.dynamic_slice_in_dim(rows, lax.axis_index("yh") * 8, 8)
    own = jnp.broadcast_to(own.reshape(1, 512, 128), (8, 512, 128))
    left = lax.all_to_all(own, "z", 0, 0, tiled=True).reshape(4096, 128)
    rights = [rows] + [
        lax.ppermute(rows, "x", [(i, (i + s) % 4) for i in range(4)]) for s in (2, 1, 3)
    ]
    where = jnp.stack([lax.axis_index("x"), lax.axis_index("c")]).astype(jnp.int32)
    own, sent = ladder_parts(products(where, amps, amps_other, rights), left, pairing)
    crossed = lax.all_to_all(sent.reshape(8, 32, 128), "z", 0, 0, tiled=True)
    parts = (own.reshape(8, 32, 128) + crossed).reshape(64, 4, 128)
    parts = lax.all_to_all(parts, GROUP, 0, 0, tiled=True)
    return finished(parts, denominator)


def solution(mesh):
    finer = Mesh(mesh.devices.reshape(SIZES), AXES)
    return jax.shard_map(
        per_device,
        mesh=finer,
        in_specs=(P(BA, DEV, None), P(None, DEV, None), P(), P(), P(), P()),
        out_specs=P(BA, DEV),
        check_vma=False,
    )
```

```python
import functools

import jax
import jax.numpy as jnp
from jax import lax
from jax.experimental import pallas as pl
from jax.experimental.pallas import tpu as pltpu
from jax.sharding import Mesh
from jax.sharding import PartitionSpec as P

NOCC = 8
AXES = ("z", "yl", "yh", "x", "c")
SIZES = (8, 4, 2, 4, 2)
BA = ("z", "yl")
DEV = ("yh", "x", "c")
GROUP = ("yh", "x", "yl", "c")
level_shift = 0.3
DSTEP = 8
STEPS = 4
VMEM_A = 52
VMEM_B = 49


def lookup(indices, table):
    choices_range = jnp.arange(table.shape[0], dtype=jnp.int32)
    return jnp.sum(
        jnp.where(indices[:, None] == choices_range[None, :], table[None, :], 0.0), axis=1
    )


def eighths_kernel(factors_ref, out_ref):
    for part in range(8):
        for r in range(2):
            chunk = factors_ref[r, :, part * 128 : (part + 1) * 128]
            for yh in range(2):
                out_ref[yh * 8 + part, r * 32 : (r + 1) * 32, :] = chunk


def in_eighths(factors):
    return pl.pallas_call(
        eighths_kernel,
        out_shape=jax.ShapeDtypeStruct((16, 64, 128), jnp.bfloat16),
        compiler_params=pltpu.CompilerParams(vmem_limit_bytes=60 * 1024 * 1024),
    )(factors)


def spread_kernel(where_ref, rows_ref, out_ref, sem):
    own = rows_ref.at[pl.ds(where_ref[2] * 8, 8)]
    copies = [pltpu.make_async_copy(own, out_ref.at[z], sem.at[z]) for z in range(8)]
    for copy in copies:
        copy.start()
    for copy in copies:
        copy.wait()


def for_each_plane(where, rows):
    return pl.pallas_call(
        spread_kernel,
        in_specs=[
            pl.BlockSpec(memory_space=pltpu.SMEM),
            pl.BlockSpec(memory_space=pl.ANY),
        ],
        out_specs=pl.BlockSpec(memory_space=pl.ANY),
        out_shape=jax.ShapeDtypeStruct((8, 8, 64, 128), jnp.bfloat16),
        scratch_shapes=[pltpu.SemaphoreType.DMA((8,))],
        compiler_params=pltpu.CompilerParams(vmem_limit_bytes=8 * 1024 * 1024),
    )(where, rows)


def product_kernel(
    where_ref, own_ref, other_ref, r0_ref, rt_ref, rp_ref, rm_ref, out_ref, amps, bmat, prods, amps_sem, b_sem, out_sem
):
    x, c = where_ref[0], where_ref[1]
    rights = [
        pltpu.make_async_copy(ref, bmat.at[(x + shift) & 3], b_sem.at[n])
        for n, (ref, shift) in enumerate(((r0_ref, 0), (rt_ref, 2), (rp_ref, 3), (rm_ref, 1)))
    ]

    def load(step, half):
        ref, place = ((own_ref, c), (other_ref, 1 - c))[half]
        return pltpu.make_async_copy(ref.at[step], amps.at[place, step], amps_sem.at[half, step])

    def store(step, yl):
        rows = pl.ds(yl * 128, 128)
        return pltpu.make_async_copy(
            prods.at[step, rows], out_ref.at[step, rows], out_sem.at[step, yl]
        )

    load(0, 0).start()
    load(0, 1).start()
    for copy in rights:
        copy.start()
    for step in range(1, STEPS):
        load(step, 0).start()
        load(step, 1).start()
    for copy in rights:
        copy.wait()

    def one_step(step, _):
        load(step, 0).wait()
        load(step, 1).wait()
        for yl in range(4):
            right = jnp.concatenate(
                [
                    jnp.concatenate(
                        [bmat[x, (yh * 4 + yl) * 2 + cc, r * 32 : r * 32 + 32, :] for r in range(2)],
                        axis=1,
                    )
                    for yh in range(2)
                    for x in range(4)
                    for cc in range(2)
                ],
                axis=0,
            )
            for cc in range(2):
                prod = jnp.dot(
                    amps[cc, step].reshape(DSTEP * 64, 512), right, preferred_element_type=jnp.float32
                ).astype(jnp.bfloat16)
                for dd in range(DSTEP):
                    lane = dd * 256 + cc * 128
                    for r in range(2):
                        b = yl * 2 + r
                        prods[step, b * 64 : (b + 1) * 64, lane : lane + 128] = prod[
                            dd * 64 : (dd + 1) * 64, r * 128 : (r + 1) * 128
                        ]
            store(step, yl).start()
        return 0

    lax.fori_loop(0, STEPS, one_step, 0)
    for step in range(STEPS):
        for yl in range(4):
            store(step, yl).wait()


def products(where, own, other, rights):
    anywhere = pl.BlockSpec(memory_space=pl.ANY)
    shape = (STEPS, 512, DSTEP * 256)
    return pl.pallas_call(
        product_kernel,
        in_specs=[pl.BlockSpec(memory_space=pltpu.SMEM)] + [anywhere] * 6,
        out_specs=pl.BlockSpec(memory_space=pltpu.HBM),
        out_shape=pltpu.HBM(shape, jnp.bfloat16),
        scratch_shapes=[
            pltpu.VMEM((2, STEPS, DSTEP, 64, 512), jnp.bfloat16),
            pltpu.VMEM((4, 16, 64, 128), jnp.bfloat16),
            pltpu.VMEM(shape, jnp.bfloat16),
            pltpu.SemaphoreType.DMA((2, STEPS)),
            pltpu.SemaphoreType.DMA((4,)),
            pltpu.SemaphoreType.DMA((STEPS, 4)),
        ],
        compiler_params=pltpu.CompilerParams(vmem_limit_bytes=VMEM_A * 1024 * 1024),
        cost_estimate=pl.CostEstimate(
            flops=2 * 4096 * 512 * 1024, bytes_accessed=14 * 1024 * 1024, transcendentals=0
        ),
    )(where, own, other, *rights)


def ladder_kernel(prod_ref, left_ref, pairing_ref, own_ref, sent_ref, prods, wide, lefts, sem):
    copies = [
        pltpu.make_async_copy(prod_ref.at[step], prods.at[step], sem.at[step])
        for step in range(STEPS)
    ]
    for copy in copies:
        copy.start()
    wide[...] = left_ref[...].astype(jnp.float32)
    total = jnp.zeros((64, 512), jnp.float32)
    for step in range(STEPS):
        for dd in range(DSTEP):
            for cc in range(2):
                lane = dd * 256 + cc * 128
                for r in range(2):
                    start = cc * 64 + r * 32 + step * DSTEP + dd
                    lefts[step, r * 32 : (r + 1) * 32, lane : lane + 128] = wide[
                        pl.ds(start, 32, stride=128), :
                    ].astype(jnp.bfloat16)
        copies[step].wait()
        total += lax.dot_general(
            lefts[step], prods[step], (((1,), (1,)), ((), ())), preferred_element_type=jnp.float32
        )
    chunks = [total[:, yl * 128 : (yl + 1) * 128] for yl in range(4)]
    for yl, rows in enumerate(chunks):
        for r in range(2):
            for z in range(8):
                own_ref[pl.ds(z * 32 + yl * 8 + r, 4, stride=2), :] = rows[
                    r * 32 + z * 4 : r * 32 + z * 4 + 4, :
                ]
    rest = jnp.concatenate(chunks, axis=0)
    paired = jnp.zeros((256, 128), jnp.float32)
    for _ in range(3):
        part = rest.astype(jnp.bfloat16)
        paired += jnp.dot(part, pairing_ref[...], preferred_element_type=jnp.float32)
        rest = rest - part.astype(jnp.float32)
    for yl in range(4):
        rows = paired[yl * 64 : (yl + 1) * 64]
        for r in range(2):
            sent_ref[pl.ds(yl * 2 + r, 32, stride=8), :] = jnp.concatenate(
                [rows[:32, r * 64 : (r + 1) * 64], rows[32:, r * 64 : (r + 1) * 64]], axis=1
            )


def ladder_parts(prods, left, pairing):
    inside = pl.BlockSpec(memory_space=pltpu.VMEM)
    return pl.pallas_call(
        ladder_kernel,
        in_specs=[pl.BlockSpec(memory_space=pltpu.HBM), inside, inside],
        out_specs=[inside] * 2,
        out_shape=[jax.ShapeDtypeStruct((256, 128), jnp.float32)] * 2,
        scratch_shapes=[
            pltpu.VMEM((STEPS, 512, DSTEP * 256), jnp.bfloat16),
            pltpu.VMEM((4096, 128), jnp.float32),
            pltpu.VMEM((STEPS, 64, DSTEP * 256), jnp.bfloat16),
            pltpu.SemaphoreType.DMA((STEPS,)),
        ],
        compiler_params=pltpu.CompilerParams(vmem_limit_bytes=VMEM_B * 1024 * 1024),
        cost_estimate=pl.CostEstimate(
            flops=2 * 64 * 64 * 8 * 8192, bytes_accessed=9 * 1024 * 1024, transcendentals=0
        ),
    )(prods, left, pairing)


def finish_kernel(parts_ref, shift_ref, out_ref):
    update = jnp.sum(parts_ref[...], axis=0) / shift_ref[...]
    for r in range(2):
        for i in range(4):
            out_ref[r : r + 1, i * 64 : (i + 1) * 64] = update[i : i + 1, r * 64 : (r + 1) * 64]


def finished(parts, shift):
    return pl.pallas_call(
        finish_kernel,
        out_shape=jax.ShapeDtypeStruct((2, 256), jnp.float32),
        compiler_params=pltpu.CompilerParams(vmem_limit_bytes=8 * 1024 * 1024),
    )(parts, shift)


def per_device(factors, amplitudes, pair_order, occ_bin, vir_bin, levels):
    swapped = pair_order % NOCC * NOCC + pair_order // NOCC
    lane = jnp.arange(128, dtype=jnp.int32)
    matches = jnp.tile(pair_order, 2)[:, None] == jnp.tile(swapped, 2)[None, :]
    pairing = (matches & (lane[:, None] // 64 == lane[None, :] // 64)).astype(jnp.bfloat16)
    virtual_energy = lookup(vir_bin, levels)
    occupied_energy = -lookup(occ_bin, levels)
    pair_energy = lookup(pair_order // NOCC, occupied_energy) + lookup(
        pair_order % NOCC, occupied_energy
    )
    left_energy = lax.dynamic_slice_in_dim(virtual_energy, lax.axis_index(DEV) * 4, 4)
    right_energy = lax.dynamic_slice_in_dim(virtual_energy, lax.axis_index(BA) * 2, 2)
    denominator = (
        right_energy[None, :, None]
        + left_energy[:, None, None]
        - pair_energy[None, None, :]
        + level_shift
    ).reshape(4, 128)

    where = jnp.stack([lax.axis_index(n) for n in ("x", "c", "yh")]).astype(jnp.int32)
    eighths = in_eighths(factors)
    eighths, sent = lax.optimization_barrier((eighths, amplitudes))
    rows = lax.all_to_all(eighths, ("yh", "yl", "c"), 0, 0, tiled=True)
    other = lax.ppermute(sent, "c", [(0, 1), (1, 0)])
    amps, amps_other = (
        t.transpose(1, 0, 2).reshape(STEPS, DSTEP, 64, 512) for t in (amplitudes, other)
    )
    rows, amps, amps_other, pairing, where = lax.optimization_barrier(
        (rows, amps, amps_other, pairing, where)
    )
    own = for_each_plane(where, rows).reshape(8, 512, 128)
    left = lax.all_to_all(own, "z", 0, 0, tiled=True).reshape(4096, 128)
    rights = [rows] + [
        lax.ppermute(rows, "x", [(i, (i + s) % 4) for i in range(4)]) for s in (2, 1, 3)
    ]
    own, sent = ladder_parts(products(where, amps, amps_other, rights), left, pairing)
    crossed = lax.all_to_all(sent.reshape(8, 32, 128), "z", 0, 0, tiled=True)
    parts = (own.reshape(8, 32, 128) + crossed).reshape(64, 4, 128)
    parts = lax.all_to_all(parts, GROUP, 0, 0, tiled=True)
    return finished(parts, denominator)


def solution(mesh):
    finer = Mesh(mesh.devices.reshape(SIZES), AXES)
    return jax.shard_map(
        per_device,
        mesh=finer,
        in_specs=(P(BA, DEV, None), P(None, DEV, None), P(), P(), P(), P()),
        out_specs=P(BA, DEV),
        check_vma=False,
    )
```

```python
import functools

import jax
import jax.numpy as jnp
from jax import lax
from jax.experimental import pallas as pl
from jax.experimental.pallas import tpu as pltpu
from jax.sharding import Mesh
from jax.sharding import PartitionSpec as P

NOCC = 8
AXES = ("z", "yl", "yh", "x", "c")
SIZES = (8, 4, 2, 4, 2)
BA = ("z", "yl")
DEV = ("yh", "x", "c")
GROUP = ("yl", "yh", "x", "c")
level_shift = 0.3
DSTEP = 8
STEPS = 4
VMEM_A = 24
VMEM_B = 49


def lookup(indices, table):
    choices_range = jnp.arange(table.shape[0], dtype=jnp.int32)
    return jnp.sum(
        jnp.where(indices[:, None] == choices_range[None, :], table[None, :], 0.0), axis=1
    )


def spread_kernel(where_ref, rows_ref, out_ref, wide, tiles, packed, sem):
    first = where_ref[2] * 8
    for n in range(8):
        wide[n * 64 : (n + 1) * 64, :] = rows_ref[first + n].astype(jnp.float32)
    for dd in range(32):
        for c in range(2):
            tile = dd * 2 + c
            for r in range(2):
                tiles[pl.ds(tile * 8 + r, 4, stride=2), :] = wide[
                    pl.ds(c * 64 + r * 32 + dd, 4, stride=128), :
                ]
            packed[:, tile * 128 : (tile + 1) * 128] = tiles[tile * 8 : (tile + 1) * 8, :].astype(
                jnp.bfloat16
            )
    copies = [pltpu.make_async_copy(packed, out_ref.at[z], sem.at[z]) for z in range(8)]
    for copy in copies:
        copy.start()
    for copy in copies:
        copy.wait()


def for_each_plane(where, rows):
    return pl.pallas_call(
        spread_kernel,
        in_specs=[
            pl.BlockSpec(memory_space=pltpu.SMEM),
            pl.BlockSpec(memory_space=pltpu.VMEM),
        ],
        out_specs=pl.BlockSpec(memory_space=pl.ANY),
        out_shape=jax.ShapeDtypeStruct((8, 8, 8192), jnp.bfloat16),
        scratch_shapes=[
            pltpu.VMEM((512, 128), jnp.float32),
            pltpu.VMEM((512, 128), jnp.float32),
            pltpu.VMEM((8, 8192), jnp.bfloat16),
            pltpu.SemaphoreType.DMA((8,)),
        ],
        compiler_params=pltpu.CompilerParams(vmem_limit_bytes=8 * 1024 * 1024),
    )(where, rows)


def product_kernel(
    where_ref, own_ref, other_ref, r0_ref, rp_ref, rm_ref, rt_ref, out_ref, amps, bmat, prods, amps_sem, b_sem, out_sem
):
    x, c = where_ref[0], where_ref[1]
    rights = [
        pltpu.make_async_copy(ref, bmat.at[(x + shift) & 3], b_sem.at[n])
        for n, (ref, shift) in enumerate(((r0_ref, 0), (rp_ref, 3), (rm_ref, 1), (rt_ref, 2)))
    ]

    def load(step, half):
        ref, place = ((own_ref, c), (other_ref, 1 - c))[half]
        return pltpu.make_async_copy(ref.at[step], amps.at[place, step], amps_sem.at[half, step])

    def store(step, yl):
        rows = pl.ds(yl * 128, 128)
        return pltpu.make_async_copy(
            prods.at[step, rows], out_ref.at[step, rows], out_sem.at[step, yl]
        )

    load(0, 0).start()
    load(0, 1).start()
    for copy in rights:
        copy.start()
    for step in range(1, STEPS):
        load(step, 0).start()
        load(step, 1).start()
    for copy in rights:
        copy.wait()

    def one_step(step, _):
        load(step, 0).wait()
        load(step, 1).wait()
        for yl in range(4):
            right = jnp.concatenate(
                [
                    jnp.concatenate(
                        [bmat[x, (yh * 4 + yl) * 2 + cc, r * 32 : r * 32 + 32, :] for r in range(2)],
                        axis=1,
                    )
                    for yh in range(2)
                    for x in range(4)
                    for cc in range(2)
                ],
                axis=0,
            )
            for cc in range(2):
                prod = jnp.dot(
                    amps[cc, step].reshape(DSTEP * 64, 512), right, preferred_element_type=jnp.float32
                ).astype(jnp.bfloat16)
                for dd in range(DSTEP):
                    lane = dd * 256 + cc * 128
                    for r in range(2):
                        b = yl * 2 + r
                        prods[step, b * 64 : (b + 1) * 64, lane : lane + 128] = prod[
                            dd * 64 : (dd + 1) * 64, r * 128 : (r + 1) * 128
                        ]
            store(step, yl).start()
        return 0

    lax.fori_loop(0, STEPS, one_step, 0)
    for step in range(STEPS):
        for yl in range(4):
            store(step, yl).wait()


def products(where, own, other, rights):
    anywhere = pl.BlockSpec(memory_space=pl.ANY)
    shape = (STEPS, 512, DSTEP * 256)
    return pl.pallas_call(
        product_kernel,
        in_specs=[pl.BlockSpec(memory_space=pltpu.SMEM)] + [anywhere] * 6,
        out_specs=pl.BlockSpec(memory_space=pltpu.HBM),
        out_shape=pltpu.HBM(shape, jnp.bfloat16),
        scratch_shapes=[
            pltpu.VMEM((2, STEPS, DSTEP, 64, 512), jnp.bfloat16),
            pltpu.VMEM((4, 16, 64, 128), jnp.bfloat16),
            pltpu.VMEM(shape, jnp.bfloat16),
            pltpu.SemaphoreType.DMA((2, STEPS)),
            pltpu.SemaphoreType.DMA((4,)),
            pltpu.SemaphoreType.DMA((STEPS, 4)),
        ],
        compiler_params=pltpu.CompilerParams(vmem_limit_bytes=VMEM_A * 1024 * 1024),
        cost_estimate=pl.CostEstimate(
            flops=2 * 4096 * 512 * 1024, bytes_accessed=14 * 1024 * 1024, transcendentals=0
        ),
    )(where, own, other, *rights)


def ladder_kernel(prod_ref, left_ref, out_ref, prods, sem):
    copies = [
        pltpu.make_async_copy(prod_ref.at[step], prods.at[step], sem.at[step])
        for step in range(STEPS)
    ]
    for copy in copies:
        copy.start()
    total = jnp.zeros((64, 512), jnp.float32)
    width = DSTEP * 256
    for step in range(STEPS):
        copies[step].wait()
        total += lax.dot_general(
            left_ref[:, step * width : (step + 1) * width],
            prods[step],
            (((1,), (1,)), ((), ())),
            preferred_element_type=jnp.float32,
        )
    for yl in range(4):
        for z in range(8):
            out_ref[z * 32 + yl * 8 : z * 32 + yl * 8 + 8, :] = total[
                z * 8 : z * 8 + 8, yl * 128 : (yl + 1) * 128
            ]


def ladder_parts(prods, left):
    return pl.pallas_call(
        ladder_kernel,
        in_specs=[
            pl.BlockSpec(memory_space=pltpu.HBM),
            pl.BlockSpec(memory_space=pltpu.VMEM),
        ],
        out_specs=pl.BlockSpec(memory_space=pltpu.VMEM),
        out_shape=jax.ShapeDtypeStruct((256, 128), jnp.float32),
        scratch_shapes=[
            pltpu.VMEM((STEPS, 512, DSTEP * 256), jnp.bfloat16),
            pltpu.SemaphoreType.DMA((STEPS,)),
        ],
        compiler_params=pltpu.CompilerParams(vmem_limit_bytes=VMEM_B * 1024 * 1024),
        cost_estimate=pl.CostEstimate(
            flops=2 * 64 * 64 * 8 * 8192, bytes_accessed=9 * 1024 * 1024, transcendentals=0
        ),
    )(prods, left)


def both_kernel(own_ref, crossed_ref, pairing_ref, out_ref, turned):
    for yl in range(4):
        rows = [crossed_ref[pl.ds(yl * 2 + r, 32, stride=8), :] for r in range(2)]
        for r in range(2):
            half = slice(r * 64, (r + 1) * 64)
            turned[pl.ds(r, 32, stride=2), :] = jnp.concatenate(
                [rows[0][:, half], rows[1][:, half]], axis=1
            )
        partnered = jnp.dot(
            turned[...],
            pairing_ref[...],
            precision=lax.Precision.HIGHEST,
            preferred_element_type=jnp.float32,
        )
        for z in range(8):
            total = own_ref[z * 32 + yl * 8 : z * 32 + yl * 8 + 8, :] + partnered[z * 8 : z * 8 + 8]
            out_ref[(yl * 8 + z) * 2] = total[:4]
            out_ref[(yl * 8 + z) * 2 + 1] = total[4:]


def both_orders(own, crossed, pairing):
    return pl.pallas_call(
        both_kernel,
        out_shape=jax.ShapeDtypeStruct((64, 4, 128), jnp.float32),
        scratch_shapes=[pltpu.VMEM((64, 128), jnp.float32)],
        compiler_params=pltpu.CompilerParams(vmem_limit_bytes=8 * 1024 * 1024),
    )(own, crossed, pairing)


def finish_kernel(parts_ref, shift_ref, out_ref):
    update = jnp.sum(parts_ref[...], axis=0) / shift_ref[...]
    for r in range(2):
        for i in range(4):
            out_ref[r : r + 1, i * 64 : (i + 1) * 64] = update[i : i + 1, r * 64 : (r + 1) * 64]


def finished(parts, shift):
    return pl.pallas_call(
        finish_kernel,
        out_shape=jax.ShapeDtypeStruct((2, 256), jnp.float32),
        compiler_params=pltpu.CompilerParams(vmem_limit_bytes=8 * 1024 * 1024),
    )(parts, shift)


def per_device(factors, amplitudes, pair_order, occ_bin, vir_bin, levels):
    swapped = pair_order % NOCC * NOCC + pair_order // NOCC
    matches = (pair_order[:, None] == swapped[None, :]).astype(jnp.float32)
    pairing = jnp.kron(jnp.eye(2, dtype=jnp.float32), matches)
    virtual_energy = lookup(vir_bin, levels)
    occupied_energy = -lookup(occ_bin, levels)
    pair_energy = lookup(pair_order // NOCC, occupied_energy) + lookup(
        pair_order % NOCC, occupied_energy
    )
    left_energy = lax.dynamic_slice_in_dim(virtual_energy, lax.axis_index(DEV) * 4, 4)
    right_energy = lax.dynamic_slice_in_dim(virtual_energy, lax.axis_index(BA) * 2, 2)
    denominator = (
        right_energy[None, :, None]
        + left_energy[:, None, None]
        - pair_energy[None, None, :]
        + level_shift
    ).reshape(4, 128)

    where = jnp.stack([lax.axis_index(n) for n in ("x", "c", "yh")]).astype(jnp.int32)
    eighths = factors.reshape(64, 8, 128).transpose(1, 0, 2)
    eighths = jnp.broadcast_to(eighths[None], (2, 8, 64, 128)).reshape(16, 64, 128)
    rows = lax.all_to_all(eighths, ("yh", "yl", "c"), 0, 0, tiled=True)
    other = lax.ppermute(amplitudes, "c", [(0, 1), (1, 0)])
    amps, amps_other = (
        t.transpose(1, 0, 2).reshape(STEPS, DSTEP, 64, 512) for t in (amplitudes, other)
    )
    left = lax.all_to_all(for_each_plane(where, rows), "z", 0, 0, tiled=True).reshape(64, 8192)
    rights = [rows] + [
        lax.ppermute(rows, "x", [(i, (i + s) % 4) for i in range(4)]) for s in (1, 3, 2)
    ]
    ladder = ladder_parts(products(where, amps, amps_other, rights), left)
    crossed = lax.all_to_all(ladder.reshape(8, 32, 128), "z", 0, 0, tiled=True)
    parts = both_orders(ladder, crossed.reshape(256, 128), pairing)
    parts = lax.all_to_all(parts, GROUP, 0, 0, tiled=True)
    return finished(parts, denominator)


def solution(mesh):
    finer = Mesh(mesh.devices.reshape(SIZES), AXES)
    return jax.shard_map(
        per_device,
        mesh=finer,
        in_specs=(P(BA, DEV, None), P(None, DEV, None), P(), P(), P(), P()),
        out_specs=P(BA, DEV),
        check_vma=False,
    )
```

```python
import functools

import jax
import jax.numpy as jnp
from jax import lax
from jax.experimental import pallas as pl
from jax.experimental.pallas import tpu as pltpu
from jax.sharding import Mesh
from jax.sharding import PartitionSpec as P

NOCC = 8
AXES = ("z", "yl", "yh", "x", "c")
SIZES = (8, 4, 2, 4, 2)
BA = ("z", "yl")
DEV = ("yh", "x", "c")
GROUP = ("yl", "yh", "x", "c")
level_shift = 0.3
DSTEP = 8
STEPS = 4
VMEM_A = 24
VMEM_B = 49


def lookup(indices, table):
    choices_range = jnp.arange(table.shape[0], dtype=jnp.int32)
    return jnp.sum(
        jnp.where(indices[:, None] == choices_range[None, :], table[None, :], 0.0), axis=1
    )


def spread_kernel(where_ref, rows_ref, out_ref, wide, tiles, packed, sem):
    first = where_ref[2] * 8
    for n in range(8):
        wide[n * 64 : (n + 1) * 64, :] = rows_ref[first + n].astype(jnp.float32)
    for dd in range(32):
        for c in range(2):
            tile = dd * 2 + c
            for r in range(2):
                tiles[pl.ds(tile * 8 + r, 4, stride=2), :] = wide[
                    pl.ds(c * 64 + r * 32 + dd, 4, stride=128), :
                ]
            packed[:, tile * 128 : (tile + 1) * 128] = tiles[tile * 8 : (tile + 1) * 8, :].astype(
                jnp.bfloat16
            )
    copies = [pltpu.make_async_copy(packed, out_ref.at[z], sem.at[z]) for z in range(8)]
    for copy in copies:
        copy.start()
    for copy in copies:
        copy.wait()


def for_each_plane(where, rows):
    return pl.pallas_call(
        spread_kernel,
        in_specs=[
            pl.BlockSpec(memory_space=pltpu.SMEM),
            pl.BlockSpec(memory_space=pltpu.VMEM),
        ],
        out_specs=pl.BlockSpec(memory_space=pl.ANY),
        out_shape=jax.ShapeDtypeStruct((8, 8, 8192), jnp.bfloat16),
        scratch_shapes=[
            pltpu.VMEM((512, 128), jnp.float32),
            pltpu.VMEM((512, 128), jnp.float32),
            pltpu.VMEM((8, 8192), jnp.bfloat16),
            pltpu.SemaphoreType.DMA((8,)),
        ],
        compiler_params=pltpu.CompilerParams(vmem_limit_bytes=8 * 1024 * 1024),
    )(where, rows)


def product_kernel(
    where_ref, own_ref, other_ref, r0_ref, rp_ref, rm_ref, rt_ref, near_ref, out_ref, amps, bmat, prods, amps_sem, b_sem, out_sem
):
    x, c = where_ref[0], where_ref[1]
    rights = [
        pltpu.make_async_copy(ref, bmat.at[(x + shift) & 3], b_sem.at[n])
        for n, (ref, shift) in enumerate(((r0_ref, 0), (rp_ref, 3), (rm_ref, 1), (rt_ref, 2)))
    ]

    def load(step, half):
        ref, place = ((own_ref, c), (other_ref, 1 - c))[half]
        return pltpu.make_async_copy(ref.at[step], amps.at[place, step], amps_sem.at[half, step])

    def store(step, yl):
        rows = pl.ds(yl * 128, 128)
        return pltpu.make_async_copy(
            prods.at[step, rows], out_ref.at[step, rows], out_sem.at[step, yl]
        )

    load(1, 0).start()
    load(1, 1).start()
    for copy in rights:
        copy.start()
    for step in (2, 3, 0):
        load(step, 0).start()
        load(step, 1).start()
    for copy in rights:
        copy.wait()

    def one_step(step, target, finish):
        load(step, 0).wait()
        load(step, 1).wait()
        for yl in range(4):
            right = jnp.concatenate(
                [
                    jnp.concatenate(
                        [bmat[x, (yh * 4 + yl) * 2 + cc, r * 32 : r * 32 + 32, :] for r in range(2)],
                        axis=1,
                    )
                    for yh in range(2)
                    for x in range(4)
                    for cc in range(2)
                ],
                axis=0,
            )
            for cc in range(2):
                prod = jnp.dot(
                    amps[cc, step].reshape(DSTEP * 64, 512), right, preferred_element_type=jnp.float32
                ).astype(jnp.bfloat16)
                for dd in range(DSTEP):
                    lane = dd * 256 + cc * 128
                    for r in range(2):
                        b = yl * 2 + r
                        target[b * 64 : (b + 1) * 64, lane : lane + 128] = prod[
                            dd * 64 : (dd + 1) * 64, r * 128 : (r + 1) * 128
                        ]
            finish(yl)

    def later(n, _):
        one_step(n + 1, prods.at[n], lambda yl: store(n, yl).start())
        return 0

    lax.fori_loop(0, STEPS - 1, later, 0)
    one_step(0, near_ref, lambda yl: None)
    for n in range(STEPS - 1):
        for yl in range(4):
            store(n, yl).wait()


def products(where, own, other, rights):
    anywhere = pl.BlockSpec(memory_space=pl.ANY)
    shape = (STEPS - 1, 512, DSTEP * 256)
    return pl.pallas_call(
        product_kernel,
        in_specs=[pl.BlockSpec(memory_space=pltpu.SMEM)] + [anywhere] * 6,
        out_specs=[pl.BlockSpec(memory_space=pltpu.VMEM), pl.BlockSpec(memory_space=pltpu.HBM)],
        out_shape=[
            jax.ShapeDtypeStruct(shape[1:], jnp.bfloat16),
            pltpu.HBM(shape, jnp.bfloat16),
        ],
        scratch_shapes=[
            pltpu.VMEM((2, STEPS, DSTEP, 64, 512), jnp.bfloat16),
            pltpu.VMEM((4, 16, 64, 128), jnp.bfloat16),
            pltpu.VMEM(shape, jnp.bfloat16),
            pltpu.SemaphoreType.DMA((2, STEPS)),
            pltpu.SemaphoreType.DMA((4,)),
            pltpu.SemaphoreType.DMA((STEPS - 1, 4)),
        ],
        compiler_params=pltpu.CompilerParams(vmem_limit_bytes=VMEM_A * 1024 * 1024),
        cost_estimate=pl.CostEstimate(
            flops=2 * 4096 * 512 * 1024, bytes_accessed=14 * 1024 * 1024, transcendentals=0
        ),
    )(where, own, other, *rights)


def ladder_kernel(near_ref, prod_ref, left_ref, out_ref, prods, sem):
    copies = [
        pltpu.make_async_copy(prod_ref.at[n], prods.at[n], sem.at[n]) for n in range(STEPS - 1)
    ]
    for copy in copies:
        copy.start()
    total = jnp.zeros((64, 512), jnp.float32)
    width = DSTEP * 256
    for step in range(STEPS):
        if step > 0:
            copies[step - 1].wait()
        total += lax.dot_general(
            left_ref[:, step * width : (step + 1) * width],
            near_ref[...] if step == 0 else prods[step - 1],
            (((1,), (1,)), ((), ())),
            preferred_element_type=jnp.float32,
        )
    for yl in range(4):
        for z in range(8):
            out_ref[z * 32 + yl * 8 : z * 32 + yl * 8 + 8, :] = total[
                z * 8 : z * 8 + 8, yl * 128 : (yl + 1) * 128
            ]


def ladder_parts(near, prods, left):
    return pl.pallas_call(
        ladder_kernel,
        in_specs=[
            pl.BlockSpec(memory_space=pltpu.VMEM),
            pl.BlockSpec(memory_space=pltpu.HBM),
            pl.BlockSpec(memory_space=pltpu.VMEM),
        ],
        out_specs=pl.BlockSpec(memory_space=pltpu.VMEM),
        out_shape=jax.ShapeDtypeStruct((256, 128), jnp.float32),
        scratch_shapes=[
            pltpu.VMEM((STEPS - 1, 512, DSTEP * 256), jnp.bfloat16),
            pltpu.SemaphoreType.DMA((STEPS - 1,)),
        ],
        compiler_params=pltpu.CompilerParams(vmem_limit_bytes=VMEM_B * 1024 * 1024),
        cost_estimate=pl.CostEstimate(
            flops=2 * 64 * 64 * 8 * 8192, bytes_accessed=9 * 1024 * 1024, transcendentals=0
        ),
    )(near, prods, left)


def both_kernel(own_ref, crossed_ref, pairing_ref, out_ref, turned):
    for yl in range(4):
        rows = [crossed_ref[pl.ds(yl * 2 + r, 32, stride=8), :] for r in range(2)]
        for r in range(2):
            half = slice(r * 64, (r + 1) * 64)
            turned[pl.ds(r, 32, stride=2), :] = jnp.concatenate(
                [rows[0][:, half], rows[1][:, half]], axis=1
            )
        partnered = jnp.dot(
            turned[...],
            pairing_ref[...],
            precision=lax.Precision.HIGHEST,
            preferred_element_type=jnp.float32,
        )
        for z in range(8):
            total = own_ref[z * 32 + yl * 8 : z * 32 + yl * 8 + 8, :] + partnered[z * 8 : z * 8 + 8]
            out_ref[(yl * 8 + z) * 2] = total[:4]
            out_ref[(yl * 8 + z) * 2 + 1] = total[4:]


def both_orders(own, crossed, pairing):
    return pl.pallas_call(
        both_kernel,
        out_shape=jax.ShapeDtypeStruct((64, 4, 128), jnp.float32),
        scratch_shapes=[pltpu.VMEM((64, 128), jnp.float32)],
        compiler_params=pltpu.CompilerParams(vmem_limit_bytes=8 * 1024 * 1024),
    )(own, crossed, pairing)


def finish_kernel(parts_ref, shift_ref, out_ref):
    update = jnp.sum(parts_ref[...], axis=0) / shift_ref[...]
    for r in range(2):
        for i in range(4):
            out_ref[r : r + 1, i * 64 : (i + 1) * 64] = update[i : i + 1, r * 64 : (r + 1) * 64]


def finished(parts, shift):
    return pl.pallas_call(
        finish_kernel,
        out_shape=jax.ShapeDtypeStruct((2, 256), jnp.float32),
        compiler_params=pltpu.CompilerParams(vmem_limit_bytes=8 * 1024 * 1024),
    )(parts, shift)


def per_device(factors, amplitudes, pair_order, occ_bin, vir_bin, levels):
    swapped = pair_order % NOCC * NOCC + pair_order // NOCC
    matches = (pair_order[:, None] == swapped[None, :]).astype(jnp.float32)
    pairing = jnp.kron(jnp.eye(2, dtype=jnp.float32), matches)
    virtual_energy = lookup(vir_bin, levels)
    occupied_energy = -lookup(occ_bin, levels)
    pair_energy = lookup(pair_order // NOCC, occupied_energy) + lookup(
        pair_order % NOCC, occupied_energy
    )
    left_energy = lax.dynamic_slice_in_dim(virtual_energy, lax.axis_index(DEV) * 4, 4)
    right_energy = lax.dynamic_slice_in_dim(virtual_energy, lax.axis_index(BA) * 2, 2)
    denominator = (
        right_energy[None, :, None]
        + left_energy[:, None, None]
        - pair_energy[None, None, :]
        + level_shift
    ).reshape(4, 128)

    where = jnp.stack([lax.axis_index(n) for n in ("x", "c", "yh")]).astype(jnp.int32)
    eighths = factors.reshape(64, 8, 128).transpose(1, 0, 2)
    eighths = jnp.broadcast_to(eighths[None], (2, 8, 64, 128)).reshape(16, 64, 128)
    rows = lax.all_to_all(eighths, ("yh", "yl", "c"), 0, 0, tiled=True)
    other = lax.ppermute(amplitudes, "c", [(0, 1), (1, 0)])
    amps, amps_other = (
        t.transpose(1, 0, 2).reshape(STEPS, DSTEP, 64, 512) for t in (amplitudes, other)
    )
    left = lax.all_to_all(for_each_plane(where, rows), "z", 0, 0, tiled=True).reshape(64, 8192)
    rights = [rows] + [
        lax.ppermute(rows, "x", [(i, (i + s) % 4) for i in range(4)]) for s in (1, 3, 2)
    ]
    ladder = ladder_parts(*products(where, amps, amps_other, rights), left)
    crossed = lax.all_to_all(ladder.reshape(8, 32, 128), "z", 0, 0, tiled=True)
    parts = both_orders(ladder, crossed.reshape(256, 128), pairing)
    parts = lax.all_to_all(parts, GROUP, 0, 0, tiled=True)
    return finished(parts, denominator)


def solution(mesh):
    finer = Mesh(mesh.devices.reshape(SIZES), AXES)
    return jax.shard_map(
        per_device,
        mesh=finer,
        in_specs=(P(BA, DEV, None), P(None, DEV, None), P(), P(), P(), P()),
        out_specs=P(BA, DEV),
        check_vma=False,
    )
```

```python
import functools

import jax
import jax.numpy as jnp
from jax import lax
from jax.experimental import pallas as pl
from jax.experimental.pallas import tpu as pltpu
from jax.sharding import Mesh
from jax.sharding import PartitionSpec as P

NOCC = 8
AXES = ("z", "yl", "yh", "x", "c")
SIZES = (8, 4, 2, 4, 2)
BA = ("z", "yl")
DEV = ("yh", "x", "c")
GROUP = ("yl", "yh", "x", "c")
level_shift = 0.3
DSTEP = 8
STEPS = 4
VMEM_A = 24
VMEM_B = 49


def lookup(indices, table):
    choices_range = jnp.arange(table.shape[0], dtype=jnp.int32)
    return jnp.sum(
        jnp.where(indices[:, None] == choices_range[None, :], table[None, :], 0.0), axis=1
    )


def spread_kernel(where_ref, rows_ref, out_ref, wide, tiles, packed, sem):
    first = where_ref[2] * 8
    for n in range(8):
        wide[n * 64 : (n + 1) * 64, :] = rows_ref[first + n].astype(jnp.float32)
    for dd in range(16):
        for c in range(2):
            tile = dd * 2 + c
            for h in range(2):
                for r in range(2):
                    tiles[pl.ds(tile * 16 + h * 8 + r, 4, stride=2), :] = wide[
                        pl.ds(c * 64 + r * 32 + h * 16 + dd, 4, stride=128), :
                    ]
            packed[:, tile * 128 : (tile + 1) * 128] = tiles[tile * 16 : (tile + 1) * 16, :].astype(
                jnp.bfloat16
            )
    copies = [pltpu.make_async_copy(packed, out_ref.at[z], sem.at[z]) for z in range(8)]
    for copy in copies:
        copy.start()
    for copy in copies:
        copy.wait()


def for_each_plane(where, rows):
    return pl.pallas_call(
        spread_kernel,
        in_specs=[
            pl.BlockSpec(memory_space=pltpu.SMEM),
            pl.BlockSpec(memory_space=pltpu.VMEM),
        ],
        out_specs=pl.BlockSpec(memory_space=pl.ANY),
        out_shape=jax.ShapeDtypeStruct((8, 16, 4096), jnp.bfloat16),
        scratch_shapes=[
            pltpu.VMEM((512, 128), jnp.float32),
            pltpu.VMEM((512, 128), jnp.float32),
            pltpu.VMEM((16, 4096), jnp.bfloat16),
            pltpu.SemaphoreType.DMA((8,)),
        ],
        compiler_params=pltpu.CompilerParams(vmem_limit_bytes=8 * 1024 * 1024),
    )(where, rows)


def product_kernel(
    where_ref, own_ref, other_ref, r0_ref, rp_ref, rm_ref, rt_ref, near_ref, out_ref, amps, bmat, prods, amps_sem, b_sem, out_sem
):
    x, c = where_ref[0], where_ref[1]
    rights = [
        pltpu.make_async_copy(ref, bmat.at[(x + shift) & 3], b_sem.at[n])
        for n, (ref, shift) in enumerate(((r0_ref, 0), (rp_ref, 3), (rm_ref, 1), (rt_ref, 2)))
    ]

    def load(step, half):
        ref, place = ((own_ref, c), (other_ref, 1 - c))[half]
        return pltpu.make_async_copy(ref.at[step], amps.at[place, step], amps_sem.at[half, step])

    def store(step, yl):
        rows = pl.ds(yl * 128, 128)
        return pltpu.make_async_copy(
            prods.at[step, rows], out_ref.at[step, rows], out_sem.at[step, yl]
        )

    load(1, 0).start()
    load(1, 1).start()
    for copy in rights:
        copy.start()
    for step in (2, 3, 0):
        load(step, 0).start()
        load(step, 1).start()
    for copy in rights:
        copy.wait()

    def one_step(step, target, finish):
        load(step, 0).wait()
        load(step, 1).wait()
        for yl in range(4):
            right = jnp.concatenate(
                [
                    jnp.concatenate(
                        [bmat[x, (yh * 4 + yl) * 2 + cc, r * 32 : r * 32 + 32, :] for r in range(2)],
                        axis=1,
                    )
                    for yh in range(2)
                    for x in range(4)
                    for cc in range(2)
                ],
                axis=0,
            )
            for cc in range(2):
                prod = jnp.dot(
                    amps[cc, step].reshape(DSTEP * 64, 512), right, preferred_element_type=jnp.float32
                ).astype(jnp.bfloat16)
                for dd in range(DSTEP):
                    lane = dd * 256 + cc * 128
                    for r in range(2):
                        b = yl * 2 + r
                        target[b * 64 : (b + 1) * 64, lane : lane + 128] = prod[
                            dd * 64 : (dd + 1) * 64, r * 128 : (r + 1) * 128
                        ]
            finish(yl)

    def later(n, _):
        one_step(n + 1, prods.at[n], lambda yl: store(n, yl).start())
        return 0

    lax.fori_loop(0, STEPS - 1, later, 0)
    one_step(0, near_ref, lambda yl: None)
    for n in range(STEPS - 1):
        for yl in range(4):
            store(n, yl).wait()


def products(where, own, other, rights):
    anywhere = pl.BlockSpec(memory_space=pl.ANY)
    shape = (STEPS - 1, 512, DSTEP * 256)
    return pl.pallas_call(
        product_kernel,
        in_specs=[pl.BlockSpec(memory_space=pltpu.SMEM)] + [anywhere] * 6,
        out_specs=[pl.BlockSpec(memory_space=pltpu.VMEM), pl.BlockSpec(memory_space=pltpu.HBM)],
        out_shape=[
            jax.ShapeDtypeStruct(shape[1:], jnp.bfloat16),
            pltpu.HBM(shape, jnp.bfloat16),
        ],
        scratch_shapes=[
            pltpu.VMEM((2, STEPS, DSTEP, 64, 512), jnp.bfloat16),
            pltpu.VMEM((4, 16, 64, 128), jnp.bfloat16),
            pltpu.VMEM(shape, jnp.bfloat16),
            pltpu.SemaphoreType.DMA((2, STEPS)),
            pltpu.SemaphoreType.DMA((4,)),
            pltpu.SemaphoreType.DMA((STEPS - 1, 4)),
        ],
        compiler_params=pltpu.CompilerParams(vmem_limit_bytes=VMEM_A * 1024 * 1024),
        cost_estimate=pl.CostEstimate(
            flops=2 * 4096 * 512 * 1024, bytes_accessed=14 * 1024 * 1024, transcendentals=0
        ),
    )(where, own, other, *rights)


def ladder_kernel(near_ref, prod_ref, left_ref, out_ref, prods, sem):
    copies = [
        pltpu.make_async_copy(prod_ref.at[n], prods.at[n], sem.at[n]) for n in range(STEPS - 1)
    ]
    for copy in copies:
        copy.start()
    total = jnp.zeros((64, 512), jnp.float32)
    width = DSTEP * 256
    for step in range(STEPS):
        if step > 0:
            copies[step - 1].wait()
        half, lane = divmod(step * width, 4096)
        both = lax.dot_general(
            left_ref[:, lane : lane + width],
            near_ref[...] if step == 0 else prods[step - 1],
            (((1,), (1,)), ((), ())),
            preferred_element_type=jnp.float32,
        )
        total += jnp.concatenate(
            [both[(z * 2 + half) * 8 : (z * 2 + half + 1) * 8] for z in range(8)], axis=0
        )
    for yl in range(4):
        for z in range(8):
            out_ref[z * 32 + yl * 8 : z * 32 + yl * 8 + 8, :] = total[
                z * 8 : z * 8 + 8, yl * 128 : (yl + 1) * 128
            ]


def ladder_parts(near, prods, left):
    return pl.pallas_call(
        ladder_kernel,
        in_specs=[
            pl.BlockSpec(memory_space=pltpu.VMEM),
            pl.BlockSpec(memory_space=pltpu.HBM),
            pl.BlockSpec(memory_space=pltpu.VMEM),
        ],
        out_specs=pl.BlockSpec(memory_space=pltpu.VMEM),
        out_shape=jax.ShapeDtypeStruct((256, 128), jnp.float32),
        scratch_shapes=[
            pltpu.VMEM((STEPS - 1, 512, DSTEP * 256), jnp.bfloat16),
            pltpu.SemaphoreType.DMA((STEPS - 1,)),
        ],
        compiler_params=pltpu.CompilerParams(vmem_limit_bytes=VMEM_B * 1024 * 1024),
        cost_estimate=pl.CostEstimate(
            flops=2 * 64 * 64 * 8 * 8192, bytes_accessed=9 * 1024 * 1024, transcendentals=0
        ),
    )(near, prods, left)


def both_kernel(own_ref, crossed_ref, pairing_ref, out_ref, turned):
    for yl in range(4):
        rows = [crossed_ref[pl.ds(yl * 2 + r, 32, stride=8), :] for r in range(2)]
        for r in range(2):
            half = slice(r * 64, (r + 1) * 64)
            turned[pl.ds(r, 32, stride=2), :] = jnp.concatenate(
                [rows[0][:, half], rows[1][:, half]], axis=1
            )
        partnered = jnp.dot(
            turned[...],
            pairing_ref[...],
            precision=lax.Precision.HIGHEST,
            preferred_element_type=jnp.float32,
        )
        for z in range(8):
            total = own_ref[z * 32 + yl * 8 : z * 32 + yl * 8 + 8, :] + partnered[z * 8 : z * 8 + 8]
            out_ref[(yl * 8 + z) * 2] = total[:4]
            out_ref[(yl * 8 + z) * 2 + 1] = total[4:]


def both_orders(own, crossed, pairing):
    return pl.pallas_call(
        both_kernel,
        out_shape=jax.ShapeDtypeStruct((64, 4, 128), jnp.float32),
        scratch_shapes=[pltpu.VMEM((64, 128), jnp.float32)],
        compiler_params=pltpu.CompilerParams(vmem_limit_bytes=8 * 1024 * 1024),
    )(own, crossed, pairing)


def finish_kernel(parts_ref, shift_ref, out_ref):
    update = jnp.sum(parts_ref[...], axis=0) / shift_ref[...]
    for r in range(2):
        for i in range(4):
            out_ref[r : r + 1, i * 64 : (i + 1) * 64] = update[i : i + 1, r * 64 : (r + 1) * 64]


def finished(parts, shift):
    return pl.pallas_call(
        finish_kernel,
        out_shape=jax.ShapeDtypeStruct((2, 256), jnp.float32),
        compiler_params=pltpu.CompilerParams(vmem_limit_bytes=8 * 1024 * 1024),
    )(parts, shift)


def per_device(factors, amplitudes, pair_order, occ_bin, vir_bin, levels):
    swapped = pair_order % NOCC * NOCC + pair_order // NOCC
    matches = (pair_order[:, None] == swapped[None, :]).astype(jnp.float32)
    pairing = jnp.kron(jnp.eye(2, dtype=jnp.float32), matches)
    virtual_energy = lookup(vir_bin, levels)
    occupied_energy = -lookup(occ_bin, levels)
    pair_energy = lookup(pair_order // NOCC, occupied_energy) + lookup(
        pair_order % NOCC, occupied_energy
    )
    left_energy = lax.dynamic_slice_in_dim(virtual_energy, lax.axis_index(DEV) * 4, 4)
    right_energy = lax.dynamic_slice_in_dim(virtual_energy, lax.axis_index(BA) * 2, 2)
    denominator = (
        right_energy[None, :, None]
        + left_energy[:, None, None]
        - pair_energy[None, None, :]
        + level_shift
    ).reshape(4, 128)

    where = jnp.stack([lax.axis_index(n) for n in ("x", "c", "yh")]).astype(jnp.int32)
    eighths = factors.reshape(64, 8, 128).transpose(1, 0, 2)
    eighths = jnp.broadcast_to(eighths[None], (2, 8, 64, 128)).reshape(16, 64, 128)
    rows = lax.all_to_all(eighths, ("yh", "yl", "c"), 0, 0, tiled=True)
    other = lax.ppermute(amplitudes, "c", [(0, 1), (1, 0)])
    amps, amps_other = (
        t.transpose(1, 0, 2).reshape(STEPS, DSTEP, 64, 512) for t in (amplitudes, other)
    )
    left = lax.all_to_all(for_each_plane(where, rows), "z", 0, 0, tiled=True).reshape(128, 4096)
    rights = [rows] + [
        lax.ppermute(rows, "x", [(i, (i + s) % 4) for i in range(4)]) for s in (1, 3, 2)
    ]
    ladder = ladder_parts(*products(where, amps, amps_other, rights), left)
    crossed = lax.all_to_all(ladder.reshape(8, 32, 128), "z", 0, 0, tiled=True)
    parts = both_orders(ladder, crossed.reshape(256, 128), pairing)
    parts = lax.all_to_all(parts, GROUP, 0, 0, tiled=True)
    return finished(parts, denominator)


def solution(mesh):
    finer = Mesh(mesh.devices.reshape(SIZES), AXES)
    return jax.shard_map(
        per_device,
        mesh=finer,
        in_specs=(P(BA, DEV, None), P(None, DEV, None), P(), P(), P(), P()),
        out_specs=P(BA, DEV),
        check_vma=False,
    )
```

```python
import functools

import jax
import jax.numpy as jnp
from jax import lax
from jax.experimental import pallas as pl
from jax.experimental.pallas import tpu as pltpu
from jax.sharding import Mesh
from jax.sharding import PartitionSpec as P

NOCC = 8
AXES = ("z", "yl", "yh", "x", "c")
SIZES = (8, 4, 2, 4, 2)
BA = ("z", "yl")
DEV = ("yh", "x", "c")
GROUP = ("yl", "yh", "x", "c")
level_shift = 0.3
DSTEP = 8
STEPS = 4
VMEM_A = 24
VMEM_B = 49


def lookup(indices, table):
    choices_range = jnp.arange(table.shape[0], dtype=jnp.int32)
    return jnp.sum(
        jnp.where(indices[:, None] == choices_range[None, :], table[None, :], 0.0), axis=1
    )


def spread_kernel(where_ref, rows_ref, out_ref, wide, tiles, packed, sem):
    first = where_ref[2] * 8
    for n in range(8):
        wide[n * 64 : (n + 1) * 64, :] = rows_ref[first + n].astype(jnp.float32)
    for dd in range(16):
        for c in range(2):
            tile = dd * 2 + c
            for h in range(2):
                for r in range(2):
                    tiles[pl.ds(tile * 16 + h * 8 + r, 4, stride=2), :] = wide[
                        pl.ds(c * 64 + r * 32 + h * 16 + dd, 4, stride=128), :
                    ]
            packed[:, tile * 128 : (tile + 1) * 128] = tiles[tile * 16 : (tile + 1) * 16, :].astype(
                jnp.bfloat16
            )
    copies = [pltpu.make_async_copy(packed, out_ref.at[z], sem.at[z]) for z in range(8)]
    for copy in copies:
        copy.start()
    for copy in copies:
        copy.wait()


def for_each_plane(where, rows):
    return pl.pallas_call(
        spread_kernel,
        in_specs=[
            pl.BlockSpec(memory_space=pltpu.SMEM),
            pl.BlockSpec(memory_space=pltpu.VMEM),
        ],
        out_specs=pl.BlockSpec(memory_space=pl.ANY),
        out_shape=jax.ShapeDtypeStruct((8, 16, 4096), jnp.bfloat16),
        scratch_shapes=[
            pltpu.VMEM((512, 128), jnp.float32),
            pltpu.VMEM((512, 128), jnp.float32),
            pltpu.VMEM((16, 4096), jnp.bfloat16),
            pltpu.SemaphoreType.DMA((8,)),
        ],
        compiler_params=pltpu.CompilerParams(vmem_limit_bytes=8 * 1024 * 1024),
    )(where, rows)


def product_kernel(
    where_ref, own_ref, other_ref, r0_ref, rp_ref, rm_ref, rt_ref, near_ref, out_ref, amps, bmat, prods, amps_sem, b_sem, out_sem
):
    x, c = where_ref[0], where_ref[1]
    rights = [
        pltpu.make_async_copy(ref, bmat.at[(x + shift) & 3], b_sem.at[n])
        for n, (ref, shift) in enumerate(((r0_ref, 0), (rp_ref, 3), (rm_ref, 1), (rt_ref, 2)))
    ]

    def load(step, half):
        ref, place = ((own_ref, c), (other_ref, 1 - c))[half]
        return pltpu.make_async_copy(ref.at[step], amps.at[place, step], amps_sem.at[half, step])

    def store(step, yl):
        rows = pl.ds(yl * 128, 128)
        return pltpu.make_async_copy(
            prods.at[step, rows], out_ref.at[step, rows], out_sem.at[step, yl]
        )

    load(1, 0).start()
    load(1, 1).start()
    for copy in rights:
        copy.start()
    for step in (2, 3, 0):
        load(step, 0).start()
        load(step, 1).start()
    for copy in rights:
        copy.wait()

    def one_step(step, target, finish):
        load(step, 0).wait()
        load(step, 1).wait()
        for yl in range(4):
            right = jnp.concatenate(
                [
                    jnp.concatenate(
                        [bmat[x, (yh * 4 + yl) * 2 + cc, r * 32 : r * 32 + 32, :] for r in range(2)],
                        axis=1,
                    )
                    for yh in range(2)
                    for x in range(4)
                    for cc in range(2)
                ],
                axis=0,
            )
            for cc in range(2):
                prod = jnp.dot(
                    amps[cc, step].reshape(DSTEP * 64, 512), right, preferred_element_type=jnp.float32
                ).astype(jnp.bfloat16)
                for dd in range(DSTEP):
                    lane = dd * 256 + cc * 128
                    for r in range(2):
                        b = yl * 2 + r
                        target[b * 64 : (b + 1) * 64, lane : lane + 128] = prod[
                            dd * 64 : (dd + 1) * 64, r * 128 : (r + 1) * 128
                        ]
            finish(yl)

    def later(n, _):
        one_step(n + 1, prods.at[n], lambda yl: store(n, yl).start())
        return 0

    lax.fori_loop(0, STEPS - 1, later, 0)
    one_step(0, near_ref, lambda yl: None)
    for n in range(STEPS - 1):
        for yl in range(4):
            store(n, yl).wait()


def products(where, own, other, rights):
    anywhere = pl.BlockSpec(memory_space=pl.ANY)
    shape = (STEPS - 1, 512, DSTEP * 256)
    return pl.pallas_call(
        product_kernel,
        in_specs=[pl.BlockSpec(memory_space=pltpu.SMEM)] + [anywhere] * 6,
        out_specs=[pl.BlockSpec(memory_space=pltpu.VMEM), pl.BlockSpec(memory_space=pltpu.HBM)],
        out_shape=[
            jax.ShapeDtypeStruct(shape[1:], jnp.bfloat16),
            pltpu.HBM(shape, jnp.bfloat16),
        ],
        scratch_shapes=[
            pltpu.VMEM((2, STEPS, DSTEP, 64, 512), jnp.bfloat16),
            pltpu.VMEM((4, 16, 64, 128), jnp.bfloat16),
            pltpu.VMEM(shape, jnp.bfloat16),
            pltpu.SemaphoreType.DMA((2, STEPS)),
            pltpu.SemaphoreType.DMA((4,)),
            pltpu.SemaphoreType.DMA((STEPS - 1, 4)),
        ],
        compiler_params=pltpu.CompilerParams(vmem_limit_bytes=VMEM_A * 1024 * 1024),
        cost_estimate=pl.CostEstimate(
            flops=2 * 4096 * 512 * 1024, bytes_accessed=14 * 1024 * 1024, transcendentals=0
        ),
    )(where, own, other, *rights)


def ladder_kernel(near_ref, prod_ref, left_ref, out_ref, prods, sem):
    copies = [
        pltpu.make_async_copy(prod_ref.at[n], prods.at[n], sem.at[n]) for n in range(STEPS - 1)
    ]
    for copy in copies:
        copy.start()
    total = jnp.zeros((64, 512), jnp.float32)
    width = DSTEP * 256
    for step in range(STEPS):
        if step > 0:
            copies[step - 1].wait()
        half, lane = divmod(step * width, 4096)
        both = lax.dot_general(
            left_ref[:, lane : lane + width],
            near_ref[...] if step == 0 else prods[step - 1],
            (((1,), (1,)), ((), ())),
            preferred_element_type=jnp.float32,
        )
        total += jnp.concatenate(
            [both[(z * 2 + half) * 8 : (z * 2 + half + 1) * 8] for z in range(8)], axis=0
        )
    for yl in range(4):
        for z in range(8):
            out_ref[z * 32 + yl * 8 : z * 32 + yl * 8 + 8, :] = total[
                z * 8 : z * 8 + 8, yl * 128 : (yl + 1) * 128
            ]


def ladder_parts(near, prods, left):
    return pl.pallas_call(
        ladder_kernel,
        in_specs=[
            pl.BlockSpec(memory_space=pltpu.VMEM),
            pl.BlockSpec(memory_space=pltpu.HBM),
            pl.BlockSpec(memory_space=pltpu.VMEM),
        ],
        out_specs=pl.BlockSpec(memory_space=pltpu.VMEM),
        out_shape=jax.ShapeDtypeStruct((256, 128), jnp.float32),
        scratch_shapes=[
            pltpu.VMEM((STEPS - 1, 512, DSTEP * 256), jnp.bfloat16),
            pltpu.SemaphoreType.DMA((STEPS - 1,)),
        ],
        compiler_params=pltpu.CompilerParams(vmem_limit_bytes=VMEM_B * 1024 * 1024),
        cost_estimate=pl.CostEstimate(
            flops=2 * 64 * 64 * 8 * 8192, bytes_accessed=9 * 1024 * 1024, transcendentals=0
        ),
    )(near, prods, left)


def both_kernel(own_ref, crossed_ref, pairing_ref, out_ref, turned):
    for yl in range(4):
        rows = [crossed_ref[pl.ds(yl * 2 + r, 32, stride=8), :] for r in range(2)]
        for r in range(2):
            half = slice(r * 64, (r + 1) * 64)
            turned[pl.ds(yl * 64 + r, 32, stride=2), :] = jnp.concatenate(
                [rows[0][:, half], rows[1][:, half]], axis=1
            )
    rest, parts = turned[...], []
    for _ in range(3):
        parts.append(rest.astype(jnp.bfloat16))
        rest = rest - parts[-1].astype(jnp.float32)
    three = jnp.dot(
        jnp.concatenate(parts, axis=0),
        pairing_ref[...].astype(jnp.bfloat16),
        preferred_element_type=jnp.float32,
    )
    partnered = three[:256] + three[256:512] + three[512:]
    for yl in range(4):
        for z in range(8):
            row = yl * 64 + z * 8
            total = own_ref[z * 32 + yl * 8 : z * 32 + yl * 8 + 8, :] + partnered[row : row + 8]
            out_ref[(yl * 8 + z) * 2] = total[:4]
            out_ref[(yl * 8 + z) * 2 + 1] = total[4:]


def both_orders(own, crossed, pairing):
    return pl.pallas_call(
        both_kernel,
        out_shape=jax.ShapeDtypeStruct((64, 4, 128), jnp.float32),
        scratch_shapes=[pltpu.VMEM((256, 128), jnp.float32)],
        compiler_params=pltpu.CompilerParams(vmem_limit_bytes=8 * 1024 * 1024),
    )(own, crossed, pairing)


def finish_kernel(parts_ref, shift_ref, out_ref):
    update = jnp.sum(parts_ref[...], axis=0) / shift_ref[...]
    for r in range(2):
        for i in range(4):
            out_ref[r : r + 1, i * 64 : (i + 1) * 64] = update[i : i + 1, r * 64 : (r + 1) * 64]


def finished(parts, shift):
    return pl.pallas_call(
        finish_kernel,
        out_shape=jax.ShapeDtypeStruct((2, 256), jnp.float32),
        compiler_params=pltpu.CompilerParams(vmem_limit_bytes=8 * 1024 * 1024),
    )(parts, shift)


def per_device(factors, amplitudes, pair_order, occ_bin, vir_bin, levels):
    swapped = pair_order % NOCC * NOCC + pair_order // NOCC
    matches = (pair_order[:, None] == swapped[None, :]).astype(jnp.float32)
    pairing = jnp.kron(jnp.eye(2, dtype=jnp.float32), matches)
    virtual_energy = lookup(vir_bin, levels)
    occupied_energy = -lookup(occ_bin, levels)
    pair_energy = lookup(pair_order // NOCC, occupied_energy) + lookup(
        pair_order % NOCC, occupied_energy
    )
    left_energy = lax.dynamic_slice_in_dim(virtual_energy, lax.axis_index(DEV) * 4, 4)
    right_energy = lax.dynamic_slice_in_dim(virtual_energy, lax.axis_index(BA) * 2, 2)
    denominator = (
        right_energy[None, :, None]
        + left_energy[:, None, None]
        - pair_energy[None, None, :]
        + level_shift
    ).reshape(4, 128)

    where = jnp.stack([lax.axis_index(n) for n in ("x", "c", "yh")]).astype(jnp.int32)
    eighths = factors.reshape(64, 8, 128).transpose(1, 0, 2)
    eighths = jnp.broadcast_to(eighths[None], (2, 8, 64, 128)).reshape(16, 64, 128)
    rows = lax.all_to_all(eighths, ("yh", "yl", "c"), 0, 0, tiled=True)
    other = lax.ppermute(amplitudes, "c", [(0, 1), (1, 0)])
    amps, amps_other = (
        t.transpose(1, 0, 2).reshape(STEPS, DSTEP, 64, 512) for t in (amplitudes, other)
    )
    left = lax.all_to_all(for_each_plane(where, rows), "z", 0, 0, tiled=True).reshape(128, 4096)
    rights = [rows] + [
        lax.ppermute(rows, "x", [(i, (i + s) % 4) for i in range(4)]) for s in (1, 3, 2)
    ]
    ladder = ladder_parts(*products(where, amps, amps_other, rights), left)
    crossed = lax.all_to_all(ladder.reshape(8, 32, 128), "z", 0, 0, tiled=True)
    parts = both_orders(ladder, crossed.reshape(256, 128), pairing)
    parts = lax.all_to_all(parts, GROUP, 0, 0, tiled=True)
    return finished(parts, denominator)


def solution(mesh):
    finer = Mesh(mesh.devices.reshape(SIZES), AXES)
    return jax.shard_map(
        per_device,
        mesh=finer,
        in_specs=(P(BA, DEV, None), P(None, DEV, None), P(), P(), P(), P()),
        out_specs=P(BA, DEV),
        check_vma=False,
    )
```

```python
import functools

import jax
import jax.numpy as jnp
from jax import lax
from jax.experimental import pallas as pl
from jax.experimental.pallas import tpu as pltpu
from jax.sharding import Mesh
from jax.sharding import PartitionSpec as P

NOCC = 8
AXES = ("z", "yl", "yh", "x", "c")
SIZES = (8, 4, 2, 4, 2)
BA = ("z", "yl")
DEV = ("yh", "x", "c")
GROUP = ("yl", "yh", "x", "c")
level_shift = 0.3
DSTEP = 8
STEPS = 4
VMEM_A = 24
VMEM_B = 49


def lookup(indices, table):
    choices_range = jnp.arange(table.shape[0], dtype=jnp.int32)
    return jnp.sum(
        jnp.where(indices[:, None] == choices_range[None, :], table[None, :], 0.0), axis=1
    )


def spread_kernel(where_ref, rows_ref, out_ref, wide, tiles, packed, sem):
    first = where_ref[2] * 8
    for n in range(8):
        wide[n * 64 : (n + 1) * 64, :] = rows_ref[first + n].astype(jnp.float32)
    for dd in range(16):
        for c in range(2):
            tile = dd * 2 + c
            for h in range(2):
                for r in range(2):
                    tiles[pl.ds(tile * 16 + h * 8 + r, 4, stride=2), :] = wide[
                        pl.ds(c * 64 + r * 32 + h * 16 + dd, 4, stride=128), :
                    ]
            packed[:, tile * 128 : (tile + 1) * 128] = tiles[tile * 16 : (tile + 1) * 16, :].astype(
                jnp.bfloat16
            )
    copies = [pltpu.make_async_copy(packed, out_ref.at[z], sem.at[z]) for z in range(8)]
    for copy in copies:
        copy.start()
    for copy in copies:
        copy.wait()


def for_each_plane(where, rows):
    return pl.pallas_call(
        spread_kernel,
        in_specs=[
            pl.BlockSpec(memory_space=pltpu.SMEM),
            pl.BlockSpec(memory_space=pltpu.VMEM),
        ],
        out_specs=pl.BlockSpec(memory_space=pl.ANY),
        out_shape=jax.ShapeDtypeStruct((8, 16, 4096), jnp.bfloat16),
        scratch_shapes=[
            pltpu.VMEM((512, 128), jnp.float32),
            pltpu.VMEM((512, 128), jnp.float32),
            pltpu.VMEM((16, 4096), jnp.bfloat16),
            pltpu.SemaphoreType.DMA((8,)),
        ],
        compiler_params=pltpu.CompilerParams(vmem_limit_bytes=8 * 1024 * 1024),
    )(where, rows)


def product_kernel(
    where_ref, own_ref, other_ref, r0_ref, rp_ref, rm_ref, rt_ref, near_ref, out_ref, amps, bmat, prods, amps_sem, b_sem, out_sem
):
    x, c = where_ref[0], where_ref[1]
    rights = [
        pltpu.make_async_copy(ref, bmat.at[(x + shift) & 3], b_sem.at[n])
        for n, (ref, shift) in enumerate(((r0_ref, 0), (rp_ref, 3), (rm_ref, 1), (rt_ref, 2)))
    ]

    def load(step, half):
        ref, place = ((own_ref, c), (other_ref, 1 - c))[half]
        return pltpu.make_async_copy(ref.at[step], amps.at[place, step], amps_sem.at[half, step])

    def store(step, yl):
        rows = pl.ds(yl * 128, 128)
        return pltpu.make_async_copy(
            prods.at[step, rows], out_ref.at[step, rows], out_sem.at[step, yl]
        )

    load(1, 0).start()
    load(1, 1).start()
    for copy in rights:
        copy.start()
    for step in (2, 3, 0):
        load(step, 0).start()
        load(step, 1).start()
    for copy in rights:
        copy.wait()

    def one_step(step, target, finish):
        load(step, 0).wait()
        load(step, 1).wait()
        for yl in range(4):
            right = jnp.concatenate(
                [
                    jnp.concatenate(
                        [bmat[x, (yh * 4 + yl) * 2 + cc, r * 32 : r * 32 + 32, :] for r in range(2)],
                        axis=1,
                    )
                    for yh in range(2)
                    for x in range(4)
                    for cc in range(2)
                ],
                axis=0,
            )
            for cc in range(2):
                prod = jnp.dot(
                    amps[cc, step].reshape(DSTEP * 64, 512), right, preferred_element_type=jnp.float32
                ).astype(jnp.bfloat16)
                for dd in range(DSTEP):
                    lane = dd * 256 + cc * 128
                    for r in range(2):
                        b = yl * 2 + r
                        target[b * 64 : (b + 1) * 64, lane : lane + 128] = prod[
                            dd * 64 : (dd + 1) * 64, r * 128 : (r + 1) * 128
                        ]
            finish(yl)

    def later(n, _):
        one_step(n + 1, prods.at[n], lambda yl: store(n, yl).start())
        return 0

    lax.fori_loop(0, STEPS - 1, later, 0)
    one_step(0, near_ref, lambda yl: None)
    for n in range(STEPS - 1):
        for yl in range(4):
            store(n, yl).wait()


def products(where, own, other, rights):
    anywhere = pl.BlockSpec(memory_space=pl.ANY)
    shape = (STEPS - 1, 512, DSTEP * 256)
    return pl.pallas_call(
        product_kernel,
        in_specs=[pl.BlockSpec(memory_space=pltpu.SMEM)] + [anywhere] * 6,
        out_specs=[pl.BlockSpec(memory_space=pltpu.VMEM), pl.BlockSpec(memory_space=pltpu.HBM)],
        out_shape=[
            jax.ShapeDtypeStruct(shape[1:], jnp.bfloat16),
            pltpu.HBM(shape, jnp.bfloat16),
        ],
        scratch_shapes=[
            pltpu.VMEM((2, STEPS, DSTEP, 64, 512), jnp.bfloat16),
            pltpu.VMEM((4, 16, 64, 128), jnp.bfloat16),
            pltpu.VMEM(shape, jnp.bfloat16),
            pltpu.SemaphoreType.DMA((2, STEPS)),
            pltpu.SemaphoreType.DMA((4,)),
            pltpu.SemaphoreType.DMA((STEPS - 1, 4)),
        ],
        compiler_params=pltpu.CompilerParams(vmem_limit_bytes=VMEM_A * 1024 * 1024),
        cost_estimate=pl.CostEstimate(
            flops=2 * 4096 * 512 * 1024, bytes_accessed=14 * 1024 * 1024, transcendentals=0
        ),
    )(where, own, other, *rights)


def ladder_kernel(near_ref, prod_ref, left_ref, out_ref, prods, sem):
    copies = [
        pltpu.make_async_copy(prod_ref.at[n], prods.at[n], sem.at[n]) for n in range(STEPS - 1)
    ]
    for copy in copies:
        copy.start()
    total = jnp.zeros((64, 512), jnp.float32)
    width = DSTEP * 256
    for step in range(STEPS):
        if step > 0:
            copies[step - 1].wait()
        half, lane = divmod(step * width, 4096)
        both = lax.dot_general(
            left_ref[:, lane : lane + width],
            near_ref[...] if step == 0 else prods[step - 1],
            (((1,), (1,)), ((), ())),
            preferred_element_type=jnp.float32,
        )
        total += jnp.concatenate(
            [both[(z * 2 + half) * 8 : (z * 2 + half + 1) * 8] for z in range(8)], axis=0
        )
    for yl in range(4):
        for z in range(8):
            out_ref[z * 32 + yl * 8 : z * 32 + yl * 8 + 8, :] = total[
                z * 8 : z * 8 + 8, yl * 128 : (yl + 1) * 128
            ]


def ladder_parts(near, prods, left):
    return pl.pallas_call(
        ladder_kernel,
        in_specs=[
            pl.BlockSpec(memory_space=pltpu.VMEM),
            pl.BlockSpec(memory_space=pltpu.HBM),
            pl.BlockSpec(memory_space=pltpu.VMEM),
        ],
        out_specs=pl.BlockSpec(memory_space=pltpu.VMEM),
        out_shape=jax.ShapeDtypeStruct((256, 128), jnp.float32),
        scratch_shapes=[
            pltpu.VMEM((STEPS - 1, 512, DSTEP * 256), jnp.bfloat16),
            pltpu.SemaphoreType.DMA((STEPS - 1,)),
        ],
        compiler_params=pltpu.CompilerParams(vmem_limit_bytes=VMEM_B * 1024 * 1024),
        cost_estimate=pl.CostEstimate(
            flops=2 * 64 * 64 * 8 * 8192, bytes_accessed=9 * 1024 * 1024, transcendentals=0
        ),
    )(near, prods, left)


def both_kernel(own_ref, crossed_ref, pairing_ref, out_ref, turned):
    for yl in range(4):
        rows = [crossed_ref[pl.ds(yl * 2 + r, 32, stride=8), :] for r in range(2)]
        for r in range(2):
            half = slice(r * 64, (r + 1) * 64)
            turned[pl.ds(yl * 64 + r, 32, stride=2), :] = jnp.concatenate(
                [rows[0][:, half], rows[1][:, half]], axis=1
            )
    rest, parts = turned[...], []
    for _ in range(3):
        parts.append(rest.astype(jnp.bfloat16))
        rest = rest - parts[-1].astype(jnp.float32)
    three = jnp.dot(
        jnp.concatenate(parts, axis=0),
        pairing_ref[...].astype(jnp.bfloat16),
        preferred_element_type=jnp.float32,
    )
    partnered = three[:256] + three[256:512] + three[512:]
    for yl in range(4):
        for z in range(8):
            row = yl * 64 + z * 8
            total = own_ref[z * 32 + yl * 8 : z * 32 + yl * 8 + 8, :] + partnered[row : row + 8]
            out_ref[(yl * 8 + z) * 2] = total[:4]
            out_ref[(yl * 8 + z) * 2 + 1] = total[4:]


def both_orders(own, crossed, pairing):
    return pl.pallas_call(
        both_kernel,
        out_shape=jax.ShapeDtypeStruct((64, 4, 128), jnp.float32),
        scratch_shapes=[pltpu.VMEM((256, 128), jnp.float32)],
        compiler_params=pltpu.CompilerParams(vmem_limit_bytes=8 * 1024 * 1024),
    )(own, crossed, pairing)


def finish_kernel(parts_ref, shift_ref, out_ref):
    update = jnp.sum(parts_ref[...], axis=0) / shift_ref[...]
    for r in range(2):
        for i in range(4):
            out_ref[r : r + 1, i * 64 : (i + 1) * 64] = update[i : i + 1, r * 64 : (r + 1) * 64]


def finished(parts, shift):
    return pl.pallas_call(
        finish_kernel,
        out_shape=jax.ShapeDtypeStruct((2, 256), jnp.float32),
        compiler_params=pltpu.CompilerParams(vmem_limit_bytes=8 * 1024 * 1024),
    )(parts, shift)


def per_device(factors, amplitudes, pair_order, occ_bin, vir_bin, levels):
    swapped = pair_order % NOCC * NOCC + pair_order // NOCC
    matches = (pair_order[:, None] == swapped[None, :]).astype(jnp.float32)
    pairing = jnp.kron(jnp.eye(2, dtype=jnp.float32), matches)
    virtual_energy = lookup(vir_bin, levels)
    occupied_energy = -lookup(occ_bin, levels)
    pair_energy = lookup(pair_order // NOCC, occupied_energy) + lookup(
        pair_order % NOCC, occupied_energy
    )
    left_energy = lax.dynamic_slice_in_dim(virtual_energy, lax.axis_index(DEV) * 4, 4)
    right_energy = lax.dynamic_slice_in_dim(virtual_energy, lax.axis_index(BA) * 2, 2)
    denominator = (
        right_energy[None, :, None]
        + left_energy[:, None, None]
        - pair_energy[None, None, :]
        + level_shift
    ).reshape(4, 128)

    where = jnp.stack([lax.axis_index(n) for n in ("x", "c", "yh")]).astype(jnp.int32)
    eighths = factors.reshape(64, 8, 128).transpose(1, 0, 2)
    eighths = jnp.broadcast_to(eighths[None], (2, 8, 64, 128)).reshape(16, 64, 128)
    rows = lax.all_to_all(eighths, ("yh", "yl", "c"), 0, 0, tiled=True)
    planes, sent = lax.optimization_barrier((for_each_plane(where, rows), amplitudes))
    left = lax.all_to_all(planes, "z", 0, 0, tiled=True).reshape(128, 4096)
    other = lax.ppermute(sent, "c", [(0, 1), (1, 0)])
    amps, amps_other = (
        t.transpose(1, 0, 2).reshape(STEPS, DSTEP, 64, 512) for t in (amplitudes, other)
    )
    rights = [rows] + [
        lax.ppermute(rows, "x", [(i, (i + s) % 4) for i in range(4)]) for s in (1, 3, 2)
    ]
    ladder = ladder_parts(*products(where, amps, amps_other, rights), left)
    crossed = lax.all_to_all(ladder.reshape(8, 32, 128), "z", 0, 0, tiled=True)
    parts = both_orders(ladder, crossed.reshape(256, 128), pairing)
    parts = lax.all_to_all(parts, GROUP, 0, 0, tiled=True)
    return finished(parts, denominator)


def solution(mesh):
    finer = Mesh(mesh.devices.reshape(SIZES), AXES)
    return jax.shard_map(
        per_device,
        mesh=finer,
        in_specs=(P(BA, DEV, None), P(None, DEV, None), P(), P(), P(), P()),
        out_specs=P(BA, DEV),
        check_vma=False,
    )
```

```python
import functools

import jax
import jax.numpy as jnp
from jax import lax
from jax.experimental import pallas as pl
from jax.experimental.pallas import tpu as pltpu
from jax.sharding import Mesh
from jax.sharding import PartitionSpec as P

NOCC = 8
AXES = ("z", "yl", "yh", "x", "c")
SIZES = (8, 4, 2, 4, 2)
BA = ("z", "yl")
DEV = ("yh", "x", "c")
GROUP = ("yl", "yh", "x", "c")
level_shift = 0.3
DSTEP = 8
STEPS = 4
VMEM_A = 24
VMEM_B = 49


def lookup(indices, table):
    choices_range = jnp.arange(table.shape[0], dtype=jnp.int32)
    return jnp.sum(
        jnp.where(indices[:, None] == choices_range[None, :], table[None, :], 0.0), axis=1
    )


def spread_kernel(where_ref, rows_ref, out_ref, wide, tiles, packed, sem):
    first = where_ref[2] * 8
    for n in range(8):
        wide[n * 64 : (n + 1) * 64, :] = rows_ref[first + n].astype(jnp.float32)
    for dd in range(16):
        for c in range(2):
            tile = dd * 2 + c
            for h in range(2):
                for r in range(2):
                    tiles[pl.ds(tile * 16 + h * 8 + r, 4, stride=2), :] = wide[
                        pl.ds(c * 64 + r * 32 + h * 16 + dd, 4, stride=128), :
                    ]
            packed[:, tile * 128 : (tile + 1) * 128] = tiles[tile * 16 : (tile + 1) * 16, :].astype(
                jnp.bfloat16
            )
    copies = [pltpu.make_async_copy(packed, out_ref.at[z], sem.at[z]) for z in range(8)]
    for copy in copies:
        copy.start()
    for copy in copies:
        copy.wait()


def for_each_plane(where, rows):
    return pl.pallas_call(
        spread_kernel,
        in_specs=[
            pl.BlockSpec(memory_space=pltpu.SMEM),
            pl.BlockSpec(memory_space=pltpu.VMEM),
        ],
        out_specs=pl.BlockSpec(memory_space=pl.ANY),
        out_shape=jax.ShapeDtypeStruct((8, 16, 4096), jnp.bfloat16),
        scratch_shapes=[
            pltpu.VMEM((512, 128), jnp.float32),
            pltpu.VMEM((512, 128), jnp.float32),
            pltpu.VMEM((16, 4096), jnp.bfloat16),
            pltpu.SemaphoreType.DMA((8,)),
        ],
        compiler_params=pltpu.CompilerParams(vmem_limit_bytes=8 * 1024 * 1024),
    )(where, rows)


def product_kernel(
    where_ref, own_ref, other_ref, r0_ref, rt_ref, rp_ref, rm_ref, near_ref, out_ref, amps, bmat, prods, amps_sem, b_sem, out_sem
):
    x, c = where_ref[0], where_ref[1]
    rights = [
        pltpu.make_async_copy(ref, bmat.at[(x + shift) & 3], b_sem.at[n])
        for n, (ref, shift) in enumerate(((r0_ref, 0), (rt_ref, 2), (rp_ref, 3), (rm_ref, 1)))
    ]

    def load(step, half):
        ref, place = ((own_ref, c), (other_ref, 1 - c))[half]
        return pltpu.make_async_copy(ref.at[step], amps.at[place, step], amps_sem.at[half, step])

    def store(step, yl):
        rows = pl.ds(yl * 128, 128)
        return pltpu.make_async_copy(
            prods.at[step, rows], out_ref.at[step, rows], out_sem.at[step, yl]
        )

    load(1, 0).start()
    load(1, 1).start()
    for copy in rights:
        copy.start()
    for step in (2, 3, 0):
        load(step, 0).start()
        load(step, 1).start()
    for copy in rights:
        copy.wait()

    def one_step(step, target, finish):
        load(step, 0).wait()
        load(step, 1).wait()
        for yl in range(4):
            right = jnp.concatenate(
                [
                    jnp.concatenate(
                        [bmat[x, (yh * 4 + yl) * 2 + cc, r * 32 : r * 32 + 32, :] for r in range(2)],
                        axis=1,
                    )
                    for yh in range(2)
                    for x in range(4)
                    for cc in range(2)
                ],
                axis=0,
            )
            for cc in range(2):
                prod = jnp.dot(
                    amps[cc, step].reshape(DSTEP * 64, 512), right, preferred_element_type=jnp.float32
                ).astype(jnp.bfloat16)
                for dd in range(DSTEP):
                    lane = dd * 256 + cc * 128
                    for r in range(2):
                        b = yl * 2 + r
                        target[b * 64 : (b + 1) * 64, lane : lane + 128] = prod[
                            dd * 64 : (dd + 1) * 64, r * 128 : (r + 1) * 128
                        ]
            finish(yl)

    def later(n, _):
        one_step(n + 1, prods.at[n], lambda yl: store(n, yl).start())
        return 0

    lax.fori_loop(0, STEPS - 1, later, 0)
    one_step(0, near_ref, lambda yl: None)
    for n in range(STEPS - 1):
        for yl in range(4):
            store(n, yl).wait()


def products(where, own, other, rights):
    anywhere = pl.BlockSpec(memory_space=pl.ANY)
    shape = (STEPS - 1, 512, DSTEP * 256)
    return pl.pallas_call(
        product_kernel,
        in_specs=[pl.BlockSpec(memory_space=pltpu.SMEM)] + [anywhere] * 6,
        out_specs=[pl.BlockSpec(memory_space=pltpu.VMEM), pl.BlockSpec(memory_space=pltpu.HBM)],
        out_shape=[
            jax.ShapeDtypeStruct(shape[1:], jnp.bfloat16),
            pltpu.HBM(shape, jnp.bfloat16),
        ],
        scratch_shapes=[
            pltpu.VMEM((2, STEPS, DSTEP, 64, 512), jnp.bfloat16),
            pltpu.VMEM((4, 16, 64, 128), jnp.bfloat16),
            pltpu.VMEM(shape, jnp.bfloat16),
            pltpu.SemaphoreType.DMA((2, STEPS)),
            pltpu.SemaphoreType.DMA((4,)),
            pltpu.SemaphoreType.DMA((STEPS - 1, 4)),
        ],
        compiler_params=pltpu.CompilerParams(vmem_limit_bytes=VMEM_A * 1024 * 1024),
        cost_estimate=pl.CostEstimate(
            flops=2 * 4096 * 512 * 1024, bytes_accessed=14 * 1024 * 1024, transcendentals=0
        ),
    )(where, own, other, *rights)


def ladder_kernel(near_ref, prod_ref, left_ref, out_ref, prods, sem):
    copies = [
        pltpu.make_async_copy(prod_ref.at[n], prods.at[n], sem.at[n]) for n in range(STEPS - 1)
    ]
    for copy in copies:
        copy.start()
    total = jnp.zeros((64, 512), jnp.float32)
    width = DSTEP * 256
    for step in range(STEPS):
        if step > 0:
            copies[step - 1].wait()
        half, lane = divmod(step * width, 4096)
        both = lax.dot_general(
            left_ref[:, lane : lane + width],
            near_ref[...] if step == 0 else prods[step - 1],
            (((1,), (1,)), ((), ())),
            preferred_element_type=jnp.float32,
        )
        total += jnp.concatenate(
            [both[(z * 2 + half) * 8 : (z * 2 + half + 1) * 8] for z in range(8)], axis=0
        )
    for yl in range(4):
        for z in range(8):
            out_ref[z * 32 + yl * 8 : z * 32 + yl * 8 + 8, :] = total[
                z * 8 : z * 8 + 8, yl * 128 : (yl + 1) * 128
            ]


def ladder_parts(near, prods, left):
    return pl.pallas_call(
        ladder_kernel,
        in_specs=[
            pl.BlockSpec(memory_space=pltpu.VMEM),
            pl.BlockSpec(memory_space=pltpu.HBM),
            pl.BlockSpec(memory_space=pltpu.VMEM),
        ],
        out_specs=pl.BlockSpec(memory_space=pltpu.VMEM),
        out_shape=jax.ShapeDtypeStruct((256, 128), jnp.float32),
        scratch_shapes=[
            pltpu.VMEM((STEPS - 1, 512, DSTEP * 256), jnp.bfloat16),
            pltpu.SemaphoreType.DMA((STEPS - 1,)),
        ],
        compiler_params=pltpu.CompilerParams(vmem_limit_bytes=VMEM_B * 1024 * 1024),
        cost_estimate=pl.CostEstimate(
            flops=2 * 64 * 64 * 8 * 8192, bytes_accessed=9 * 1024 * 1024, transcendentals=0
        ),
    )(near, prods, left)


def both_kernel(own_ref, crossed_ref, pairing_ref, out_ref, turned):
    for yl in range(4):
        rows = [crossed_ref[pl.ds(yl * 2 + r, 32, stride=8), :] for r in range(2)]
        for r in range(2):
            half = slice(r * 64, (r + 1) * 64)
            turned[pl.ds(yl * 64 + r, 32, stride=2), :] = jnp.concatenate(
                [rows[0][:, half], rows[1][:, half]], axis=1
            )
    rest, parts = turned[...], []
    for _ in range(3):
        parts.append(rest.astype(jnp.bfloat16))
        rest = rest - parts[-1].astype(jnp.float32)
    three = jnp.dot(
        jnp.concatenate(parts, axis=0),
        pairing_ref[...].astype(jnp.bfloat16),
        preferred_element_type=jnp.float32,
    )
    partnered = three[:256] + three[256:512] + three[512:]
    for yl in range(4):
        for z in range(8):
            row = yl * 64 + z * 8
            total = own_ref[z * 32 + yl * 8 : z * 32 + yl * 8 + 8, :] + partnered[row : row + 8]
            out_ref[(yl * 8 + z) * 2] = total[:4]
            out_ref[(yl * 8 + z) * 2 + 1] = total[4:]


def both_orders(own, crossed, pairing):
    return pl.pallas_call(
        both_kernel,
        out_shape=jax.ShapeDtypeStruct((64, 4, 128), jnp.float32),
        scratch_shapes=[pltpu.VMEM((256, 128), jnp.float32)],
        compiler_params=pltpu.CompilerParams(vmem_limit_bytes=8 * 1024 * 1024),
    )(own, crossed, pairing)


def finish_kernel(parts_ref, shift_ref, out_ref):
    update = jnp.sum(parts_ref[...], axis=0) / shift_ref[...]
    for r in range(2):
        for i in range(4):
            out_ref[r : r + 1, i * 64 : (i + 1) * 64] = update[i : i + 1, r * 64 : (r + 1) * 64]


def finished(parts, shift):
    return pl.pallas_call(
        finish_kernel,
        out_shape=jax.ShapeDtypeStruct((2, 256), jnp.float32),
        compiler_params=pltpu.CompilerParams(vmem_limit_bytes=8 * 1024 * 1024),
    )(parts, shift)


def per_device(factors, amplitudes, pair_order, occ_bin, vir_bin, levels):
    swapped = pair_order % NOCC * NOCC + pair_order // NOCC
    matches = (pair_order[:, None] == swapped[None, :]).astype(jnp.float32)
    pairing = jnp.kron(jnp.eye(2, dtype=jnp.float32), matches)
    virtual_energy = lookup(vir_bin, levels)
    occupied_energy = -lookup(occ_bin, levels)
    pair_energy = lookup(pair_order // NOCC, occupied_energy) + lookup(
        pair_order % NOCC, occupied_energy
    )
    left_energy = lax.dynamic_slice_in_dim(virtual_energy, lax.axis_index(DEV) * 4, 4)
    right_energy = lax.dynamic_slice_in_dim(virtual_energy, lax.axis_index(BA) * 2, 2)
    denominator = (
        right_energy[None, :, None]
        + left_energy[:, None, None]
        - pair_energy[None, None, :]
        + level_shift
    ).reshape(4, 128)

    where = jnp.stack([lax.axis_index(n) for n in ("x", "c", "yh")]).astype(jnp.int32)
    eighths = factors.reshape(64, 8, 128).transpose(1, 0, 2)
    eighths = jnp.broadcast_to(eighths[None], (2, 8, 64, 128)).reshape(16, 64, 128)
    rows = lax.all_to_all(eighths, ("yh", "yl", "c"), 0, 0, tiled=True)
    other = lax.ppermute(amplitudes, "c", [(0, 1), (1, 0)])
    amps, amps_other = (
        t.transpose(1, 0, 2).reshape(STEPS, DSTEP, 64, 512) for t in (amplitudes, other)
    )
    left = lax.all_to_all(for_each_plane(where, rows), "z", 0, 0, tiled=True).reshape(128, 4096)
    rights = [rows] + [
        lax.ppermute(rows, "x", [(i, (i + s) % 4) for i in range(4)]) for s in (2, 1, 3)
    ]
    ladder = ladder_parts(*products(where, amps, amps_other, rights), left)
    crossed = lax.all_to_all(ladder.reshape(8, 32, 128), "z", 0, 0, tiled=True)
    parts = both_orders(ladder, crossed.reshape(256, 128), pairing)
    parts = lax.all_to_all(parts, GROUP, 0, 0, tiled=True)
    return finished(parts, denominator)


def solution(mesh):
    finer = Mesh(mesh.devices.reshape(SIZES), AXES)
    return jax.shard_map(
        per_device,
        mesh=finer,
        in_specs=(P(BA, DEV, None), P(None, DEV, None), P(), P(), P(), P()),
        out_specs=P(BA, DEV),
        check_vma=False,
    )
```
